256 devices in a mesh: section: 8 (over z_lo, core), dp: 32 (over x, y, z_hi).
Axes of the slice: x: 4, y: 4, z: 8 (z_hi: 2, z_lo: 4; z = z_hi * 4 + z_lo), core: 2. Of those that a mesh axis runs over, the one named last changes fastest.
Arguments:
- outputs: bfloat16 [8, 4096, 6144], P('section', 'dp'), may hold values from -6 to 6
- cotangents: bfloat16 [8, 4, 4096, 6144], P('section', None, 'dp'), may hold values from -6 to 6
- gain: float32 [8, 6144], P('section'), may hold values from 0.25 to 1.75
- w_in: bfloat16 [8, 6144, 32], P('section'), may hold values from -0.3125 to 0.3125
- w_out: bfloat16 [8, 32, 32], P('section'), may hold values from -1 to 1
Outputs:
- grad_outputs: bfloat16 [8, 4096, 6144], P('section', 'dp')
- grad_w_in: float32 [8, 6144, 32], P('section')
- grad_w_out: float32 [8, 32, 32], P('section')
- grad_gain: float32 [8, 6144], P('section')
The draws below stay inside these ranges and needn't reach their ends.
All inputs are finite; a program needn't handle non-finite values.
Results may differ from the reference program's by a relative error of at most 0.03.
Values may be sent and summed in bfloat16 or wider, within the bound.
A program may use at most 128 MiB of HBM per device.

```python
import jax
import jax.numpy as jnp
from jax import lax

D = 6144
STREAMS = 4
LAYERS = 8
GATE = 32
TOKENS = 4096


def level_of(rng, extent, cuts, low, largest):
    factor_of = 1.0
    for position, blocks in cuts:
        draws = jax.random.uniform(jax.random.fold_in(jax.random.fold_in(rng, 6), position), (blocks,), jnp.float32, low / len(cuts), largest / len(cuts))
        factor_of = factor_of * jnp.repeat(jnp.exp(draws), extent[position] // blocks).reshape((-1,) + (1,) * (len(extent) - 1 - position))
    return factor_of


def normal_values(own_key, shape, spread, reach, shards=(), held_as=jnp.bfloat16):
    array = jax.random.normal(own_key, shape, jnp.float32) * spread
    if len(shards) > 0:
        array = level_of(own_key, shape, shards, -0.22, 0.18) * array
    return jnp.clip(array, min=-reach, max=reach).astype(held_as)


def setup_inputs(seed: int = 0) -> dict:
    keys = jax.random.split(jax.random.key(seed), 6)
    outputs = normal_values(keys[0], (LAYERS, TOKENS, D), 1.0, 6.0, ((0, 8), (1, 32)))
    cotangents = normal_values(keys[1], (LAYERS, STREAMS, TOKENS, D), 1.0, 6.0, ((0, 8), (2, 32)))
    gain = jnp.clip(1.0 + 0.15 * jax.random.normal(keys[2], (LAYERS, D), jnp.float32), 0.25, 1.75)
    w_in = normal_values(keys[3], (LAYERS, D, GATE), (D // 16) ** -0.5, 0.3125, ((0, 8),))
    w_out = normal_values(keys[4], (LAYERS, GATE, STREAMS * LAYERS), GATE ** -0.5, 1.0, ((0, 8),))
    return dict(outputs=outputs, cotangents=cotangents, gain=gain, w_in=w_in, w_out=w_out)


def gelu_back(pre, dhid):
    return jax.vjp(lambda v: jax.nn.gelu(v, approximate=True), pre)[1](dhid)[0]

def reference(outputs, cotangents, gain, w_in, w_out):
    layers = outputs.shape[0]
    tok = outputs.shape[1]
    whole_x = outputs.astype(jnp.float32)
    summed = jnp.zeros(outputs.shape, jnp.float32)
    gate_grads, win_grads, wout_grads, gain_grads = ([], [], [], [])
    for s in range(layers):
        x = whole_x[s]
        rinv = lax.rsqrt(lax.optimization_barrier(jnp.mean(x * x, axis=-1, keepdims=True)) + 1e-06)
        normed = x * rinv
        hnorm = (normed * gain[s]).astype(jnp.bfloat16)
        pre = jnp.dot(hnorm, w_in[s], preferred_element_type=jnp.float32)
        hid = jax.nn.gelu(pre, approximate=True).astype(jnp.bfloat16)
        keep = (jnp.arange(layers) <= s).astype(jnp.float32)
        mixw = jnp.dot(hid, w_out[s], preferred_element_type=jnp.float32).reshape(tok, 4, layers) * keep
        dys = cotangents[s].astype(jnp.float32)
        dmix = jnp.einsum('ctd,jtd->tcj', dys, whole_x, precision=lax.Precision.HIGHEST) * keep
        part = jnp.einsum('tcj,ctd->jtd', mixw, dys, precision=lax.Precision.HIGHEST).astype(jnp.bfloat16)
        summed = summed + lax.optimization_barrier(part).astype(jnp.float32)
        dflat = dmix.reshape(tok, 4 * layers).astype(jnp.bfloat16)
        wout_grads.append(jnp.dot(hid.T, dflat, preferred_element_type=jnp.float32))
        dhid = jnp.dot(dflat, w_out[s].T, preferred_element_type=jnp.float32)
        dpre = gelu_back(pre, dhid).astype(jnp.bfloat16)
        win_grads.append(jnp.dot(hnorm.T, dpre, preferred_element_type=jnp.float32))
        dh = jnp.dot(dpre, w_in[s].T, preferred_element_type=jnp.float32)
        gain_grads.append(lax.optimization_barrier(jnp.sum(dh * normed, axis=0)))
        dn = dh * gain[s]
        gate_grads.append(rinv * (dn - normed * lax.optimization_barrier(jnp.mean(dn * normed, axis=-1, keepdims=True))))
    grad_outputs = (summed + jnp.stack(gate_grads)).astype(jnp.bfloat16)
    return (grad_outputs, jnp.stack(win_grads), jnp.stack(wout_grads), jnp.stack(gain_grads))
```

```python
import functools

import jax
import jax.numpy as jnp
from jax import lax
from jax.experimental import pallas as pl
from jax.experimental.pallas import tpu as pltpu
from jax.sharding import PartitionSpec as P

ND = 12
NB = 1
LAG = 3
PF = 3
PF_TOP = 6
MESH = pl.DeviceIdType.MESH
F32 = jnp.float32
BF16 = jnp.bfloat16
C0 = 0.7978845608028654
C1 = 0.044715


def gelu(v):
    return 0.5 * v * (1.0 + jnp.tanh(C0 * (v + C1 * v * v * v)))


def gelu_slope(v):
    t = jnp.tanh(C0 * (v + C1 * v * v * v))
    return 0.5 * (1.0 + t) + 0.5 * v * (1.0 - t * t) * (C0 * (1.0 + 3.0 * C1 * v * v))


def nt(a, b):
    return lax.dot_general(a, b, (((1,), (1,)), ((), ())), preferred_element_type=F32)


def tn(a, b):
    return lax.dot_general(a, b, (((0,), (0,)), ((), ())), preferred_element_type=F32)


def iota(shape, dim):
    return lax.broadcasted_iota(jnp.int32, shape, dim)


def kernel(
    nq, x_ref, cot_ref, gain_ref, win_ref, wout_ref,
    out_ref, gwin_ref, gwout_ref, ggain_ref,
    X, HN, OUT, GG, G, C, CB, PB, R, SR, PS, A, A3, ACC, ACC3,
    PRE, RI, MS, WF, WS, W3, DMT, DM, DMB, D3X, DP, WO,
    PK, RB, ZF, ZS, ZR, AG,
    x_sem, out_sem, lg_sem, lc_sem, sg_s, sg_r, sc_s, sc_r, up_s, up_r, fw_s, fw_r,
    dn_s, dn_r, cb_s, cb_r, ss_s, ss_r, w_s, w_r, w3_s, w3_r, dm_s, dm_r, d3_s, d3_r,
    rs_s, rs_r, z_s, z_r, ag_s, ag_r,
):
    D = x_ref.shape[1]
    DC = D // ND
    CW = D // nq
    s = lax.axis_index("section")
    dp = lax.axis_index("dp")
    k = s // 2
    c = s % 2
    q = dp // 2
    zh = dp % 2
    sib = s + 1 - 2 * c
    top = k == 3
    below_top = k < 3

    def half(h):
        return pl.ds(pl.multiple_of(h * 64, 64), 64)

    def cols(d):
        return pl.ds(pl.multiple_of(d * DC, 128), DC)

    def wide(p):
        return pl.ds(pl.multiple_of(p * CW, 128), CW)

    def send(src, dst, ss, rs, to):
        return pltpu.make_async_remote_copy(
            src_ref=src, dst_ref=dst, send_sem=ss, recv_sem=rs, device_id=to, device_id_type=MESH
        )

    def sec(n):
        return {"section": n}

    def load_x():
        return pltpu.make_async_copy(x_ref, X, x_sem)

    def load_g(d):
        return pltpu.make_async_copy(x_ref.at[half(c), cols(d)], G.at[d, s], lg_sem.at[d])

    def load_c(d):
        return pltpu.make_async_copy(
            cot_ref.at[:, half(c), cols(d)], C.at[d, pl.ds(4 * c, 4)], lc_sem.at[d]
        )

    def sib_g(d):
        return send(x_ref.at[half(1 - c), cols(d)], G.at[d, s], sg_s.at[d], sg_r.at[d], sec(sib))

    def sib_c(d):
        return send(
            cot_ref.at[:, half(1 - c), cols(d)], C.at[d, pl.ds(4 * c, 4)], sc_s.at[d], sc_r.at[d], sec(sib)
        )

    def up_own(d, h, source):
        to = jnp.minimum(2 * k + 2 + h, 7)
        return send(x_ref.at[half(h), cols(d)], G.at[d, s], up_s.at[d, h], up_r.at[d, source], sec(to))

    def up_fwd(d, m):
        pair = pl.ds(2 * m, 2)
        return send(
            G.at[d, pair], G.at[d, pair], fw_s.at[d, m], fw_r.at[d, m], sec(jnp.minimum(s + 2, 7))
        )

    def down(d, m):
        pair = pl.ds(2 * m, 2)
        return send(
            PB.at[d, pair], R.at[d, pair], dn_s.at[d, m], dn_r.at[d, m], sec(jnp.maximum(s - 2, 0))
        )

    def hand(d, h, source):
        return send(
            cot_ref.at[:, half(h), cols(d)], CB.at[d, pl.ds(4 * c, 4)], cb_s.at[d, h], cb_r.at[d, source],
            sec(4 + h),
        )

    def sib_s(d):
        return send(PB.at[d, sib], SR.at[d], ss_s.at[d], ss_r.at[d], sec(sib))

    def sib_w():
        return send(WF.at[half(1 - c)], WS.at[c], w_s, w_r, sec(sib))

    def top_w(h, source):
        return send(WF.at[half(h)], W3.at[c], w3_s.at[h], w3_r.at[source], sec(4 + h))

    def sib_dm():
        return send(DMT.at[1 - c], DM.at[c], dm_s, dm_r, sec(sib))

    def top_dm(cc, source):
        return send(D3X.at[cc], DMB.at[c], d3_s.at[cc], d3_r.at[source], sec(6 + cc))

    def peer(p):
        return {"dp": 2 * p + zh}

    def rs(p, source):
        return send(PK.at[p], RB.at[q], rs_s.at[p], rs_r.at[source], peer(p))

    def swap():
        return send(ZS, ZR, z_s, z_r, {"dp": dp + 1 - 2 * zh})

    def ag(p, source):
        return send(AG.at[q], AG.at[q], ag_s.at[p], ag_r.at[source], peer(p))

    def around(o):
        return lax.rem(q + o, nq)

    load_x().start()

    def first_loads(d, carry):
        load_c(d).start()
        load_g(d).start()
        return carry

    lax.fori_loop(0, PF, first_loads, 0)

    barrier = pltpu.get_barrier_semaphore()

    def greet(to):
        pl.semaphore_signal(barrier, inc=1, device_id=to, device_id_type=MESH)

    greet(sec(sib))
    for h in range(2):

        @pl.when(below_top)
        def _():
            greet(sec(jnp.minimum(2 * k + 2 + h, 7)))

        @pl.when(k > 0)
        def _():
            greet(sec(jnp.maximum(2 * k - 2 + h, 0)))

    def greet_peer(o, carry):
        greet(peer(around(o)))
        return carry

    lax.fori_loop(1, nq, greet_peer, 0)
    greet({"dp": dp + 1 - 2 * zh})
    sides = jnp.where(below_top, 2, 0) + jnp.where(k > 0, 2, 0)
    pl.semaphore_wait(barrier, nq + 1 + sides)

    def goes_up(d):
        return jnp.logical_and(below_top, jnp.logical_or(k < 2, d >= NB))

    def start_up(d):
        @pl.when(goes_up(d))
        def _():
            for h in range(2):
                up_own(d, h, c).start()

    @pl.when(top)
    def _():
        for d in range(NB):
            for h in range(2):
                hand(d, h, c).start()

    def first_sends(d, carry):
        start_up(d)
        sib_c(d).start()
        sib_g(d).start()
        return carry

    lax.fori_loop(0, PF, first_sends, 0)
    ahead = jnp.where(k == 2, PF_TOP, PF)

    def more_up(d, carry):
        start_up(d)
        return carry

    lax.fori_loop(PF, ahead, more_up, 0)

    @pl.when(top)
    def _():
        for d in range(NB):
            for j in range(6):
                G[d, j] = jnp.zeros((64, DC), BF16)

    load_x().wait()
    step = D // 6

    def norm_rows(r, carry):
        rows = pl.ds(pl.multiple_of(r * 16, 16), 16)
        total = jnp.zeros((16, 1), F32)
        for p in range(6):
            v = X[rows, p * step : (p + 1) * step].astype(F32)
            total = total + jnp.sum(v * v, axis=1, keepdims=True)
        rinv = lax.rsqrt(total * (1.0 / D) + 1e-06)
        RI[rows, :] = rinv
        for p in range(6):
            at = slice(p * step, (p + 1) * step)
            HN[rows, at] = (X[rows, at].astype(F32) * rinv * gain_ref[:, at]).astype(BF16)
        return carry

    lax.fori_loop(0, 8, norm_rows, 0)
    pre = nt(HN[...], win_ref[...])
    PRE[...] = pre
    hid = gelu(pre).astype(BF16)
    mixw = jnp.dot(hid, wout_ref[...], preferred_element_type=F32)
    mixw = jnp.where((iota((128, 32), 1) & 7) <= s, mixw, 0.0)
    WF[...] = jnp.zeros((128, 128), BF16)
    WF[:, 0:32] = mixw.astype(BF16)
    sib_w().start()

    @pl.when(top)
    def _():
        for h in range(2):
            top_w(h, c).start()

    WS[c] = WF[half(c), :]
    for g in range(2):
        ACC[g] = jnp.zeros((256, 256), F32)
    sib_w().wait_recv()

    def spread(W, A):
        row = iota((256, 128), 0)
        lane = iota((256, 128), 1)
        pick = jnp.logical_and(lane < 32, (lane & 7) == (row >> 5))
        srow = iota((128, 256), 0)
        scol = iota((128, 256), 1)
        same = (iota((256, 256), 0) & 31) == (iota((256, 256), 1) & 31)
        for g in range(2):
            total = jnp.zeros((256, 256), F32)
            for cc in range(2):
                w = W[cc, 32 * g : 32 * g + 32, :].astype(F32)
                w = jnp.where(pick, jnp.concatenate([w] * 8, axis=0), 0.0).astype(BF16)
                place = jnp.logical_and(srow < 32, (scol >> 5) == 4 * cc + (srow >> 3))
                total = total + jnp.dot(w, jnp.where(place, 1.0, 0.0).astype(BF16), preferred_element_type=F32)
            A[g] = jnp.where(same, total, 0.0).astype(BF16)

    spread(WS, A)

    def group(ref, d, g):
        return ref[d, :, 32 * g : 32 * g + 32, :].reshape(256, DC)

    def stage_part(d):
        handed = d < NB
        for g in range(2):
            PS[g] = jnp.dot(A[g], group(C, d, g), preferred_element_type=F32)

        @pl.when(jnp.logical_and(k == 2, handed))
        def _():
            for a in range(2):
                hand(d, 0, a).wait_recv()
            for g in range(2):
                PS[g] = PS[g] + jnp.dot(A3[g], group(CB, d, g), preferred_element_type=F32)
                ACC3[g] = ACC3[g] + nt(group(CB, d, g), group(G, d, g))

        takes = jnp.logical_and(below_top, jnp.logical_or(k < 2, d >= NB))
        for m in range(4):

            def keep(with_r):
                for g in range(2):
                    rows = slice(32 * g, 32 * g + 32)
                    own = PS[g, 64 * m : 64 * m + 64, :].reshape(2, 32, DC)
                    if with_r:
                        own = own + R[d, 2 * m : 2 * m + 2, rows, :].astype(F32)
                    PB[d, 2 * m : 2 * m + 2, rows, :] = own.astype(BF16)

            if m < 3:

                @pl.when(jnp.logical_and(m <= k, takes))
                def _():
                    down(d, m).wait_recv()
                    keep(True)

            @pl.when(jnp.logical_and(m <= k, jnp.logical_not(takes)))
            def _():
                keep(False)

            if m < 3:

                @pl.when(jnp.logical_and(m < k, jnp.logical_or(below_top, d >= NB)))
                def _():
                    down(d, m).start()

            @pl.when(m == k)
            def _():
                sib_s(d).start()

    def stage_gather(d):
        for m in (2, 1, 0):

            @pl.when(jnp.logical_and(m < k, jnp.logical_or(below_top, d >= NB)))
            def _():
                @pl.when(m == k - 1)
                def _():
                    for a in range(2):
                        up_own(d, 0, a).wait_recv()

                if m < 2:

                    @pl.when(m < k - 1)
                    def _():
                        up_fwd(d, m).wait_recv()

                    @pl.when(goes_up(d))
                    def _():
                        up_fwd(d, m).start()

    def stage_dmix(d):
        load_g(d).wait()
        sib_g(d).wait_recv()
        for g in range(2):
            ACC[g] = ACC[g] + nt(group(C, d, g), group(G, d, g))

    def extract(acc, low, rise, into):
        row = iota((256, 256), 0)
        col = iota((256, 256), 1)
        ok = jnp.logical_and((row & 31) == (col & 31), (col >> 5) <= low + rise * (row >> 7))
        srow = iota((256, 128), 0)
        lane = iota((256, 128), 1)
        place = jnp.where(jnp.logical_and(lane < 32, (lane & 7) == (srow >> 5)), 1.0, 0.0)
        mine = (lane >> 3) == ((srow >> 5) & 3)
        for g in range(2):
            v = jnp.where(ok, acc[g], 0.0)
            v = jnp.dot(v, place, precision=lax.Precision.HIGHEST, preferred_element_type=F32)
            v = jnp.where(mine, v, 0.0)
            for cc in range(2):
                into[cc, 32 * g : 32 * g + 32, :] = sum(
                    v[128 * cc + 32 * st : 128 * cc + 32 * st + 32] for st in range(4)
                )

    def stage_grads():
        extract(ACC, 2 * k, 1, DMT)
        sib_dm().start()
        DM[c] = DMT[c]
        sib_dm().wait_recv()

        @pl.when(top)
        def _():
            for a in range(2):
                top_dm(0, a).wait_recv()
            DM[...] = DM[...] + DMB[...]

        dflat = DM[...].reshape(128, 128)[:, 0:32].astype(BF16)
        pre = PRE[...]
        dpre = (gelu_slope(pre) * nt(dflat, wout_ref[...])).astype(BF16)
        DP[...] = dpre
        WO[...] = jnp.zeros((32, CW), F32)
        WO[:, 0:32] = tn(gelu(pre).astype(BF16), dflat)
        MS[...] = jnp.zeros((128, 1), F32)

        def pack(o, carry):
            p = around(o)
            at = wide(p)
            dh = jnp.dot(DP[...], win_ref[:, at], preferred_element_type=F32)
            t = dh * (X[:, at].astype(F32) * RI[...])
            MS[...] = MS[...] + jnp.sum(t * gain_ref[:, at], axis=1, keepdims=True)
            PK[p, 0:32, :] = tn(DP[...], HN[:, at]).astype(BF16)
            rid = iota((16, CW), 0)
            per = 32 // nq
            tile = jnp.where(rid == 0, jnp.sum(t, axis=0, keepdims=True), 0.0)
            for e in range(per):
                tile = jnp.where(rid == 1 + e, WO[pl.ds(per * p + e, 1), :], tile)
            PK[p, 32:48, :] = tile.astype(BF16)

            @pl.when(o < nq)
            def _():
                rs(p, q).start()

            return carry

        lax.fori_loop(1, nq + 1, pack, 0)

        def gate(p, carry):
            at = wide(p)
            dn = jnp.dot(DP[...], win_ref[:, at], preferred_element_type=F32) * gain_ref[:, at]
            normed = X[:, at].astype(F32) * RI[...]
            GG[:, at] = RI[...] * (dn - normed * (MS[...] * (1.0 / D)))
            return carry

        lax.fori_loop(0, nq, gate, 0)

    def stage_sum():
        ZF[...] = PK[q].astype(F32)

        def add(o, carry):
            p = around(o)
            rs(0, p).wait_recv()
            ZF[...] = ZF[...] + RB[p].astype(F32)
            return carry

        lax.fori_loop(1, nq, add, 0)
        ZS[...] = ZF[...].astype(BF16)
        swap().start()

    def stage_share():
        swap().wait_recv()
        AG[q] = (ZS[...].astype(F32) + ZR[...].astype(F32)).astype(BF16)

        def give(o, carry):
            ag(around(o), q).start()
            return carry

        lax.fori_loop(1, nq, give, 0)

    @pl.when(k == 2)
    def _():
        for a in range(2):
            top_w(0, a).wait_recv()
        spread(W3, A3)
        for g in range(2):
            ACC3[g] = jnp.zeros((256, 256), F32)

    lead_part = jnp.where(top, 0, LAG)
    lead_dmix = jnp.where(top, LAG, 0)
    tail = ND + lead_dmix

    def body(i, carry):
        @pl.when(i + PF < ND)
        def _():
            d = i + PF
            load_c(d).start()
            load_g(d).start()
            sib_c(d).start()
            sib_g(d).start()

        @pl.when(i + ahead < ND)
        def _():
            start_up(i + ahead)

        @pl.when(i < ND)
        def _():
            load_c(i).wait()
            sib_c(i).wait_recv()

        @pl.when(jnp.logical_and(k == 2, i == NB + LAG))
        def _():
            extract(ACC3, 5, 0, D3X)
            for cc in range(2):
                top_dm(cc, c).start()

        pl.when(i == tail)(stage_grads)
        pl.when(i == tail + 1)(stage_sum)
        pl.when(i == tail + 2)(stage_share)
        d = i - lead_part

        @pl.when(jnp.logical_and(d >= 0, d < ND))
        def _():
            stage_part(d)

        e = i - lead_dmix

        @pl.when(jnp.logical_and(e >= 0, e < ND))
        def _():
            stage_gather(e)
            stage_dmix(e)

        return carry

    lax.fori_loop(0, ND + LAG + 3, body, 0)

    def finish(d, carry):
        sib_s(d).wait_recv()
        at = cols(d)
        OUT[half(c), at] = (PB[d, s].astype(F32) + GG[half(c), at]).astype(BF16)
        OUT[half(1 - c), at] = (SR[d].astype(F32) + GG[half(1 - c), at]).astype(BF16)
        return carry

    lax.fori_loop(0, ND, finish, 0)
    store = pltpu.make_async_copy(OUT, out_ref, out_sem)
    store.start()

    def unpack(o, carry):
        p = around(o)

        @pl.when(o < nq)
        def _():
            ag(0, p).wait_recv()

        at = wide(p)
        gwin_ref[:, at] = AG[p, 0:32, :].astype(F32)
        extra = AG[p, 32:48, :].astype(F32)
        ggain_ref[:, at] = extra[0:1]
        per = 32 // nq
        for e in range(per):
            gwout_ref[pl.ds(per * p + e, 1), :] = extra[1 + e : 2 + e, 0:32]
        return carry

    lax.fori_loop(1, nq + 1, unpack, 0)

    def drain(d, carry):
        sib_c(d).wait_send()
        sib_g(d).wait_send()
        sib_s(d).wait_send()

        @pl.when(goes_up(d))
        def _():
            for h in range(2):
                up_own(d, h, c).wait_send()
            for m in range(2):

                @pl.when(m < k)
                def _():
                    up_fwd(d, m).wait_send()

        for m in range(3):

            @pl.when(jnp.logical_and(m < k, jnp.logical_or(below_top, d >= NB)))
            def _():
                down(d, m).wait_send()

        return carry

    lax.fori_loop(0, ND, drain, 0)
    sib_w().wait_send()
    sib_dm().wait_send()

    @pl.when(top)
    def _():
        for h in range(2):
            top_w(h, c).wait_send()
            for d in range(NB):
                hand(d, h, c).wait_send()

    @pl.when(k == 2)
    def _():
        for cc in range(2):
            top_dm(cc, c).wait_send()

    def drain_peer(o, carry):
        p = around(o)
        rs(p, q).wait_send()
        ag(p, q).wait_send()
        return carry

    lax.fori_loop(1, nq, drain_peer, 0)
    swap().wait_send()
    store.wait()


def shards(outputs, cotangents, gain, w_in, w_out):
    D = outputs.shape[2]
    nq = lax.axis_size("dp") // 2
    DC = D // ND
    CW = D // nq
    dma = pltpu.SemaphoreType.DMA
    any_space = pl.BlockSpec(memory_space=pl.ANY)
    vmem = pl.BlockSpec(memory_space=pltpu.VMEM)
    scratch = [
        pltpu.VMEM((128, D), BF16),
        pltpu.VMEM((128, D), BF16),
        pltpu.VMEM((128, D), BF16),
        pltpu.VMEM((128, D), F32),
        pltpu.VMEM((ND, 8, 64, DC), BF16),
        pltpu.VMEM((ND, 8, 64, DC), BF16),
        pltpu.VMEM((NB, 8, 64, DC), BF16),
        pltpu.VMEM((ND, 8, 64, DC), BF16),
        pltpu.VMEM((ND, 6, 64, DC), BF16),
        pltpu.VMEM((ND, 64, DC), BF16),
        pltpu.VMEM((2, 256, DC), F32),
        pltpu.VMEM((2, 256, 256), BF16),
        pltpu.VMEM((2, 256, 256), BF16),
        pltpu.VMEM((2, 256, 256), F32),
        pltpu.VMEM((2, 256, 256), F32),
        pltpu.VMEM((128, 32), F32),
        pltpu.VMEM((128, 1), F32),
        pltpu.VMEM((128, 1), F32),
        pltpu.VMEM((128, 128), BF16),
        pltpu.VMEM((2, 64, 128), BF16),
        pltpu.VMEM((2, 64, 128), BF16),
        pltpu.VMEM((2, 64, 128), F32),
        pltpu.VMEM((2, 64, 128), F32),
        pltpu.VMEM((2, 64, 128), F32),
        pltpu.VMEM((2, 64, 128), F32),
        pltpu.VMEM((128, 32), BF16),
        pltpu.VMEM((32, CW), F32),
        pltpu.VMEM((nq, 48, CW), BF16),
        pltpu.VMEM((nq, 48, CW), BF16),
        pltpu.VMEM((48, CW), F32),
        pltpu.VMEM((48, CW), BF16),
        pltpu.VMEM((48, CW), BF16),
        pltpu.VMEM((nq, 48, CW), BF16),
        dma, dma, dma((ND,)), dma((ND,)),
        dma((ND,)), dma((ND,)), dma((ND,)), dma((ND,)),
        dma((ND, 2)), dma((ND, 2)), dma((ND, 2)), dma((ND, 2)),
        dma((ND, 3)), dma((ND, 3)), dma((NB, 2)), dma((NB, 2)),
        dma((ND,)), dma((ND,)), dma, dma, dma((2,)), dma((2,)),
        dma, dma, dma((2,)), dma((2,)),
        dma((nq,)), dma((nq,)), dma, dma, dma((nq,)), dma((nq,)),
    ]
    grad, gwin, gwout, ggain = pl.pallas_call(
        functools.partial(kernel, nq),
        out_shape=(
            jax.ShapeDtypeStruct((128, D), BF16),
            jax.ShapeDtypeStruct((32, D), F32),
            jax.ShapeDtypeStruct((32, 32), F32),
            jax.ShapeDtypeStruct((1, D), F32),
        ),
        in_specs=[any_space, any_space, vmem, vmem, vmem],
        out_specs=(any_space, vmem, vmem, vmem),
        scratch_shapes=scratch,
        name="dense_back",
        compiler_params=pltpu.CompilerParams(
            collective_id=0, has_side_effects=True, vmem_limit_bytes=56 << 20
        ),
    )(outputs[0], cotangents[0], gain, w_in[0].T, w_out[0])
    return grad[None], gwin.T[None], gwout[None], ggain


def solution(mesh):
    placed = (
        P("section", "dp", None),
        P("section", None, "dp", None),
        P("section", None),
        P("section", None, None),
        P("section", None, None),
    )
    return jax.shard_map(
        shards,
        mesh=mesh,
        in_specs=placed,
        out_specs=(
            P("section", "dp", None),
            P("section", None, None),
            P("section", None, None),
            P("section", None),
        ),
        check_vma=False,
    )
```

```python
import functools

import jax
import jax.numpy as jnp
from jax import lax
from jax.experimental import pallas as pl
from jax.experimental.pallas import tpu as pltpu
from jax.sharding import PartitionSpec as P

ND = 12
NB = 1
PF = 3
PF_TOP = 6
MESH = pl.DeviceIdType.MESH
F32 = jnp.float32
BF16 = jnp.bfloat16
C0 = 0.7978845608028654
C1 = 0.044715


def gelu(v):
    return 0.5 * v * (1.0 + jnp.tanh(C0 * (v + C1 * v * v * v)))


def gelu_slope(v):
    t = jnp.tanh(C0 * (v + C1 * v * v * v))
    return 0.5 * (1.0 + t) + 0.5 * v * (1.0 - t * t) * (C0 * (1.0 + 3.0 * C1 * v * v))


def nt(a, b):
    return lax.dot_general(a, b, (((1,), (1,)), ((), ())), preferred_element_type=F32)


def tn(a, b):
    return lax.dot_general(a, b, (((0,), (0,)), ((), ())), preferred_element_type=F32)


def iota(shape, dim):
    return lax.broadcasted_iota(jnp.int32, shape, dim)


def kernel(
    nq, x_ref, cot_ref, gain_ref, win_ref, wout_ref,
    out_ref, gwin_ref, gwout_ref, ggain_ref,
    X, HN, OUT, GG, G, C, CB, PB, R, SR, PS, A, A3, ACC, ACC3,
    PRE, RI, MS, WF, WS, W3, DMT, DM, DMB, D3X, DP, WO,
    PK, RB, ZF, ZS, ZR, AG,
    x_sem, out_sem, lg_sem, lc_sem, sg_s, sg_r, sc_s, sc_r, up_s, up_r, fw_s, fw_r,
    dn_s, dn_r, cb_s, cb_r, ss_s, ss_r, w_s, w_r, w3_s, w3_r, dm_s, dm_r, d3_s, d3_r,
    rs_s, rs_r, z_s, z_r, ag_s, ag_r,
):
    D = x_ref.shape[1]
    DC = D // ND
    CW = D // nq
    s = lax.axis_index("section")
    dp = lax.axis_index("dp")
    k = s // 2
    c = s % 2
    q = dp // 2
    zh = dp % 2
    sib = s + 1 - 2 * c
    top = k == 3
    below_top = k < 3

    def half(h):
        return pl.ds(pl.multiple_of(h * 64, 64), 64)

    def cols(d):
        return pl.ds(pl.multiple_of(d * DC, 128), DC)

    def wide(p):
        return pl.ds(pl.multiple_of(p * CW, 128), CW)

    def send(src, dst, ss, rs, to):
        return pltpu.make_async_remote_copy(
            src_ref=src, dst_ref=dst, send_sem=ss, recv_sem=rs, device_id=to, device_id_type=MESH
        )

    def sec(n):
        return {"section": n}

    def load_x():
        return pltpu.make_async_copy(x_ref, X, x_sem)

    def load_g(d):
        return pltpu.make_async_copy(x_ref.at[half(c), cols(d)], G.at[d, s], lg_sem.at[d])

    def load_c(d):
        return pltpu.make_async_copy(
            cot_ref.at[:, half(c), cols(d)], C.at[d, pl.ds(4 * c, 4)], lc_sem.at[d]
        )

    def sib_g(d):
        return send(x_ref.at[half(1 - c), cols(d)], G.at[d, s], sg_s.at[d], sg_r.at[d], sec(sib))

    def sib_c(d):
        return send(
            cot_ref.at[:, half(1 - c), cols(d)], C.at[d, pl.ds(4 * c, 4)], sc_s.at[d], sc_r.at[d], sec(sib)
        )

    def up_own(d, h, source):
        to = jnp.minimum(2 * k + 2 + h, 7)
        return send(x_ref.at[half(h), cols(d)], G.at[d, s], up_s.at[d, h], up_r.at[d, source], sec(to))

    def up_fwd(d, m):
        pair = pl.ds(2 * m, 2)
        return send(
            G.at[d, pair], G.at[d, pair], fw_s.at[d, m], fw_r.at[d, m], sec(jnp.minimum(s + 2, 7))
        )

    def down(d, m):
        pair = pl.ds(2 * m, 2)
        return send(
            PB.at[d, pair], R.at[d, pair], dn_s.at[d, m], dn_r.at[d, m], sec(jnp.maximum(s - 2, 0))
        )

    def hand(d, h, source):
        return send(
            cot_ref.at[:, half(h), cols(d)], CB.at[d, pl.ds(4 * c, 4)], cb_s.at[d, h], cb_r.at[d, source],
            sec(4 + h),
        )

    def sib_s(d):
        return send(PB.at[d, sib], SR.at[d], ss_s.at[d], ss_r.at[d], sec(sib))

    def sib_w():
        return send(WF.at[half(1 - c)], WS.at[c], w_s, w_r, sec(sib))

    def top_w(h, source):
        return send(WF.at[half(h)], W3.at[c], w3_s.at[h], w3_r.at[source], sec(4 + h))

    def sib_dm():
        return send(DMT.at[1 - c], DM.at[c], dm_s, dm_r, sec(sib))

    def top_dm(cc, source):
        return send(D3X.at[cc], DMB.at[c], d3_s.at[cc], d3_r.at[source], sec(6 + cc))

    def peer(p):
        return {"dp": 2 * p + zh}

    def rs(p, source):
        return send(PK.at[p], RB.at[q], rs_s.at[p], rs_r.at[source], peer(p))

    def swap():
        return send(ZS, ZR, z_s, z_r, {"dp": dp + 1 - 2 * zh})

    def ag(p, source):
        return send(AG.at[q], AG.at[q], ag_s.at[p], ag_r.at[source], peer(p))

    def around(o):
        return lax.rem(q + o, nq)

    load_x().start()

    def first_loads(d, carry):
        load_c(d).start()
        load_g(d).start()
        return carry

    lax.fori_loop(0, PF, first_loads, 0)

    barrier = pltpu.get_barrier_semaphore()

    def greet(to):
        pl.semaphore_signal(barrier, inc=1, device_id=to, device_id_type=MESH)

    greet(sec(sib))
    for h in range(2):

        @pl.when(below_top)
        def _():
            greet(sec(jnp.minimum(2 * k + 2 + h, 7)))

        @pl.when(k > 0)
        def _():
            greet(sec(jnp.maximum(2 * k - 2 + h, 0)))

    def greet_peer(o, carry):
        greet(peer(around(o)))
        return carry

    lax.fori_loop(1, nq, greet_peer, 0)
    greet({"dp": dp + 1 - 2 * zh})
    sides = jnp.where(below_top, 2, 0) + jnp.where(k > 0, 2, 0)
    pl.semaphore_wait(barrier, nq + 1 + sides)

    def goes_up(d):
        return jnp.logical_and(below_top, jnp.logical_or(k < 2, d >= NB))

    def start_up(d):
        @pl.when(goes_up(d))
        def _():
            for h in range(2):
                up_own(d, h, c).start()

    @pl.when(top)
    def _():
        for d in range(NB):
            for h in range(2):
                hand(d, h, c).start()

    def first_sends(d, carry):
        start_up(d)
        sib_c(d).start()
        sib_g(d).start()
        return carry

    lax.fori_loop(0, PF, first_sends, 0)
    ahead = jnp.where(k == 2, PF_TOP, PF)

    def more_up(d, carry):
        start_up(d)
        return carry

    lax.fori_loop(PF, ahead, more_up, 0)

    speed = jnp.where(k == 0, 12, jnp.where(k == 1, 6, 3))

    def used(i):
        return jnp.minimum(ND, jnp.where(top, i + 1, ((i + 1) * speed) // 2))

    @pl.when(top)
    def _():
        for d in range(NB):
            for j in range(6):
                G[d, j] = jnp.zeros((64, DC), BF16)

    load_x().wait()
    step = D // 6

    def norm_rows(r, carry):
        rows = pl.ds(pl.multiple_of(r * 16, 16), 16)
        total = jnp.zeros((16, 1), F32)
        for p in range(6):
            v = X[rows, p * step : (p + 1) * step].astype(F32)
            total = total + jnp.sum(v * v, axis=1, keepdims=True)
        rinv = lax.rsqrt(total * (1.0 / D) + 1e-06)
        RI[rows, :] = rinv
        for p in range(6):
            at = slice(p * step, (p + 1) * step)
            HN[rows, at] = (X[rows, at].astype(F32) * rinv * gain_ref[:, at]).astype(BF16)
        return carry

    lax.fori_loop(0, 8, norm_rows, 0)
    pre = nt(HN[...], win_ref[...])
    PRE[...] = pre
    hid = gelu(pre).astype(BF16)
    mixw = jnp.dot(hid, wout_ref[...], preferred_element_type=F32)
    mixw = jnp.where((iota((128, 32), 1) & 7) <= s, mixw, 0.0)
    WF[...] = jnp.zeros((128, 128), BF16)
    WF[:, 0:32] = mixw.astype(BF16)
    sib_w().start()

    @pl.when(top)
    def _():
        for h in range(2):
            top_w(h, c).start()

    WS[c] = WF[half(c), :]
    for g in range(2):
        ACC[g] = jnp.zeros((256, 256), F32)
    sib_w().wait_recv()

    def spread(W, A):
        row = iota((256, 128), 0)
        lane = iota((256, 128), 1)
        pick = jnp.logical_and(lane < 32, (lane & 7) == (row >> 5))
        srow = iota((128, 256), 0)
        scol = iota((128, 256), 1)
        same = (iota((256, 256), 0) & 31) == (iota((256, 256), 1) & 31)
        for g in range(2):
            total = jnp.zeros((256, 256), F32)
            for cc in range(2):
                w = W[cc, 32 * g : 32 * g + 32, :].astype(F32)
                w = jnp.where(pick, jnp.concatenate([w] * 8, axis=0), 0.0).astype(BF16)
                place = jnp.logical_and(srow < 32, (scol >> 5) == 4 * cc + (srow >> 3))
                total = total + jnp.dot(w, jnp.where(place, 1.0, 0.0).astype(BF16), preferred_element_type=F32)
            A[g] = jnp.where(same, total, 0.0).astype(BF16)

    spread(WS, A)

    def group(ref, d, g):
        return ref[d, :, 32 * g : 32 * g + 32, :].reshape(256, DC)

    def stage_part(d):
        handed = d < NB

        @pl.when(top)
        def _():
            load_c(d).wait()
            sib_c(d).wait_recv()

        for g in range(2):
            PS[g] = jnp.dot(A[g], group(C, d, g), preferred_element_type=F32)

        @pl.when(jnp.logical_and(k == 2, handed))
        def _():
            for a in range(2):
                hand(d, 0, a).wait_recv()
            for g in range(2):
                PS[g] = PS[g] + jnp.dot(A3[g], group(CB, d, g), preferred_element_type=F32)
                ACC3[g] = ACC3[g] + nt(group(CB, d, g), group(G, d, g))

        takes = jnp.logical_and(below_top, jnp.logical_or(k < 2, d >= NB))
        for m in range(4):

            def keep(with_r):
                for g in range(2):
                    rows = slice(32 * g, 32 * g + 32)
                    own = PS[g, 64 * m : 64 * m + 64, :].reshape(2, 32, DC)
                    if with_r:
                        own = own + R[d, 2 * m : 2 * m + 2, rows, :].astype(F32)
                    PB[d, 2 * m : 2 * m + 2, rows, :] = own.astype(BF16)

            if m < 3:

                @pl.when(jnp.logical_and(m <= k, takes))
                def _():
                    down(d, m).wait_recv()
                    keep(True)

            @pl.when(jnp.logical_and(m <= k, jnp.logical_not(takes)))
            def _():
                keep(False)

            if m < 3:

                @pl.when(jnp.logical_and(m < k, jnp.logical_or(below_top, d >= NB)))
                def _():
                    down(d, m).start()

            @pl.when(m == k)
            def _():
                sib_s(d).start()

    def stage_gather(d):
        for m in (2, 1, 0):

            @pl.when(jnp.logical_and(m < k, jnp.logical_or(below_top, d >= NB)))
            def _():
                @pl.when(m == k - 1)
                def _():
                    for a in range(2):
                        up_own(d, 0, a).wait_recv()

                if m < 2:

                    @pl.when(m < k - 1)
                    def _():
                        up_fwd(d, m).wait_recv()

                    @pl.when(goes_up(d))
                    def _():
                        up_fwd(d, m).start()

    def stage_dmix(d):
        @pl.when(below_top)
        def _():
            load_c(d).wait()
            sib_c(d).wait_recv()

        load_g(d).wait()
        sib_g(d).wait_recv()
        for g in range(2):
            ACC[g] = ACC[g] + nt(group(C, d, g), group(G, d, g))

    def extract(acc, low, rise, into):
        row = iota((256, 256), 0)
        col = iota((256, 256), 1)
        ok = jnp.logical_and((row & 31) == (col & 31), (col >> 5) <= low + rise * (row >> 7))
        srow = iota((256, 128), 0)
        lane = iota((256, 128), 1)
        place = jnp.where(jnp.logical_and(lane < 32, (lane & 7) == (srow >> 5)), 1.0, 0.0)
        mine = (lane >> 3) == ((srow >> 5) & 3)
        for g in range(2):
            v = jnp.where(ok, acc[g], 0.0)
            v = jnp.dot(v, place, precision=lax.Precision.HIGHEST, preferred_element_type=F32)
            v = jnp.where(mine, v, 0.0)
            for cc in range(2):
                into[cc, 32 * g : 32 * g + 32, :] = sum(
                    v[128 * cc + 32 * st : 128 * cc + 32 * st + 32] for st in range(4)
                )

    def stage_grads():
        extract(ACC, 2 * k, 1, DMT)
        sib_dm().start()
        DM[c] = DMT[c]
        sib_dm().wait_recv()

        @pl.when(top)
        def _():
            for a in range(2):
                top_dm(0, a).wait_recv()
            DM[...] = DM[...] + DMB[...]

        dflat = DM[...].reshape(128, 128)[:, 0:32].astype(BF16)
        pre = PRE[...]
        dpre = (gelu_slope(pre) * nt(dflat, wout_ref[...])).astype(BF16)
        DP[...] = dpre
        WO[...] = jnp.zeros((32, CW), F32)
        WO[:, 0:32] = tn(gelu(pre).astype(BF16), dflat)
        MS[...] = jnp.zeros((128, 1), F32)

        def pack(o, carry):
            p = around(o)
            at = wide(p)
            dh = jnp.dot(DP[...], win_ref[:, at], preferred_element_type=F32)
            t = dh * (X[:, at].astype(F32) * RI[...])
            MS[...] = MS[...] + jnp.sum(t * gain_ref[:, at], axis=1, keepdims=True)
            PK[p, 0:32, :] = tn(DP[...], HN[:, at]).astype(BF16)
            rid = iota((16, CW), 0)
            per = 32 // nq
            tile = jnp.where(rid == 0, jnp.sum(t, axis=0, keepdims=True), 0.0)
            for e in range(per):
                tile = jnp.where(rid == 1 + e, WO[pl.ds(per * p + e, 1), :], tile)
            PK[p, 32:48, :] = tile.astype(BF16)

            @pl.when(o < nq)
            def _():
                rs(p, q).start()

            return carry

        lax.fori_loop(1, nq + 1, pack, 0)

        def gate(p, carry):
            at = wide(p)
            dn = jnp.dot(DP[...], win_ref[:, at], preferred_element_type=F32) * gain_ref[:, at]
            normed = X[:, at].astype(F32) * RI[...]
            GG[:, at] = RI[...] * (dn - normed * (MS[...] * (1.0 / D)))
            return carry

        lax.fori_loop(0, nq, gate, 0)

    def stage_sum():
        ZF[...] = PK[q].astype(F32)

        def add(o, carry):
            p = around(o)
            rs(0, p).wait_recv()
            ZF[...] = ZF[...] + RB[p].astype(F32)
            return carry

        lax.fori_loop(1, nq, add, 0)
        ZS[...] = ZF[...].astype(BF16)
        swap().start()

    def stage_share():
        swap().wait_recv()
        AG[q] = (ZS[...].astype(F32) + ZR[...].astype(F32)).astype(BF16)

        def give(o, carry):
            ag(around(o), q).start()
            return carry

        lax.fori_loop(1, nq, give, 0)

    @pl.when(k == 2)
    def _():
        for a in range(2):
            top_w(0, a).wait_recv()
        spread(W3, A3)
        for g in range(2):
            ACC3[g] = jnp.zeros((256, 256), F32)

    lead_part = jnp.where(top, 0, 1)
    tail = jnp.where(top, 2 * ND, (2 * ND + 2) // 3)

    def body(i, carry):
        def loads(d, carry):
            load_c(d).start()
            load_g(d).start()
            sib_c(d).start()
            sib_g(d).start()
            return carry

        lax.fori_loop(jnp.minimum(ND, used(i - 1) + PF), jnp.minimum(ND, used(i) + PF), loads, 0)
        lax.fori_loop(jnp.minimum(ND, used(i - 1) + ahead), jnp.minimum(ND, used(i) + ahead), more_up, 0)

        @pl.when(jnp.logical_and(k == 2, i == NB + 1))
        def _():
            extract(ACC3, 5, 0, D3X)
            for cc in range(2):
                top_dm(cc, c).start()

        pl.when(i == tail)(stage_grads)
        pl.when(i == tail + 1)(stage_sum)
        pl.when(i == tail + 2)(stage_share)
        d = i - lead_part

        @pl.when(jnp.logical_and(d >= 0, d < ND))
        def _():
            stage_part(d)

        def dots(d, carry):
            stage_gather(d)
            stage_dmix(d)
            return carry

        lo = jnp.where(top, jnp.clip(i - ND, 0, ND), used(i - 1))
        hi = jnp.where(top, jnp.clip(i - ND + 1, 0, ND), used(i))
        lax.fori_loop(lo, hi, dots, 0)
        return carry

    lax.fori_loop(0, 2 * ND + 3, body, 0)

    def finish(d, carry):
        sib_s(d).wait_recv()
        at = cols(d)
        OUT[half(c), at] = (PB[d, s].astype(F32) + GG[half(c), at]).astype(BF16)
        OUT[half(1 - c), at] = (SR[d].astype(F32) + GG[half(1 - c), at]).astype(BF16)
        return carry

    lax.fori_loop(0, ND, finish, 0)
    store = pltpu.make_async_copy(OUT, out_ref, out_sem)
    store.start()

    def unpack(o, carry):
        p = around(o)

        @pl.when(o < nq)
        def _():
            ag(0, p).wait_recv()

        at = wide(p)
        gwin_ref[:, at] = AG[p, 0:32, :].astype(F32)
        extra = AG[p, 32:48, :].astype(F32)
        ggain_ref[:, at] = extra[0:1]
        per = 32 // nq
        for e in range(per):
            gwout_ref[pl.ds(per * p + e, 1), :] = extra[1 + e : 2 + e, 0:32]
        return carry

    lax.fori_loop(1, nq + 1, unpack, 0)

    def drain(d, carry):
        sib_c(d).wait_send()
        sib_g(d).wait_send()
        sib_s(d).wait_send()

        @pl.when(goes_up(d))
        def _():
            for h in range(2):
                up_own(d, h, c).wait_send()
            for m in range(2):

                @pl.when(m < k)
                def _():
                    up_fwd(d, m).wait_send()

        for m in range(3):

            @pl.when(jnp.logical_and(m < k, jnp.logical_or(below_top, d >= NB)))
            def _():
                down(d, m).wait_send()

        return carry

    lax.fori_loop(0, ND, drain, 0)
    sib_w().wait_send()
    sib_dm().wait_send()

    @pl.when(top)
    def _():
        for h in range(2):
            top_w(h, c).wait_send()
            for d in range(NB):
                hand(d, h, c).wait_send()

    @pl.when(k == 2)
    def _():
        for cc in range(2):
            top_dm(cc, c).wait_send()

    def drain_peer(o, carry):
        p = around(o)
        rs(p, q).wait_send()
        ag(p, q).wait_send()
        return carry

    lax.fori_loop(1, nq, drain_peer, 0)
    swap().wait_send()
    store.wait()


def shards(outputs, cotangents, gain, w_in, w_out):
    D = outputs.shape[2]
    nq = lax.axis_size("dp") // 2
    DC = D // ND
    CW = D // nq
    dma = pltpu.SemaphoreType.DMA
    any_space = pl.BlockSpec(memory_space=pl.ANY)
    vmem = pl.BlockSpec(memory_space=pltpu.VMEM)
    scratch = [
        pltpu.VMEM((128, D), BF16),
        pltpu.VMEM((128, D), BF16),
        pltpu.VMEM((128, D), BF16),
        pltpu.VMEM((128, D), F32),
        pltpu.VMEM((ND, 8, 64, DC), BF16),
        pltpu.VMEM((ND, 8, 64, DC), BF16),
        pltpu.VMEM((NB, 8, 64, DC), BF16),
        pltpu.VMEM((ND, 8, 64, DC), BF16),
        pltpu.VMEM((ND, 6, 64, DC), BF16),
        pltpu.VMEM((ND, 64, DC), BF16),
        pltpu.VMEM((2, 256, DC), F32),
        pltpu.VMEM((2, 256, 256), BF16),
        pltpu.VMEM((2, 256, 256), BF16),
        pltpu.VMEM((2, 256, 256), F32),
        pltpu.VMEM((2, 256, 256), F32),
        pltpu.VMEM((128, 32), F32),
        pltpu.VMEM((128, 1), F32),
        pltpu.VMEM((128, 1), F32),
        pltpu.VMEM((128, 128), BF16),
        pltpu.VMEM((2, 64, 128), BF16),
        pltpu.VMEM((2, 64, 128), BF16),
        pltpu.VMEM((2, 64, 128), F32),
        pltpu.VMEM((2, 64, 128), F32),
        pltpu.VMEM((2, 64, 128), F32),
        pltpu.VMEM((2, 64, 128), F32),
        pltpu.VMEM((128, 32), BF16),
        pltpu.VMEM((32, CW), F32),
        pltpu.VMEM((nq, 48, CW), BF16),
        pltpu.VMEM((nq, 48, CW), BF16),
        pltpu.VMEM((48, CW), F32),
        pltpu.VMEM((48, CW), BF16),
        pltpu.VMEM((48, CW), BF16),
        pltpu.VMEM((nq, 48, CW), BF16),
        dma, dma, dma((ND,)), dma((ND,)),
        dma((ND,)), dma((ND,)), dma((ND,)), dma((ND,)),
        dma((ND, 2)), dma((ND, 2)), dma((ND, 2)), dma((ND, 2)),
        dma((ND, 3)), dma((ND, 3)), dma((NB, 2)), dma((NB, 2)),
        dma((ND,)), dma((ND,)), dma, dma, dma((2,)), dma((2,)),
        dma, dma, dma((2,)), dma((2,)),
        dma((nq,)), dma((nq,)), dma, dma, dma((nq,)), dma((nq,)),
    ]
    grad, gwin, gwout, ggain = pl.pallas_call(
        functools.partial(kernel, nq),
        out_shape=(
            jax.ShapeDtypeStruct((128, D), BF16),
            jax.ShapeDtypeStruct((32, D), F32),
            jax.ShapeDtypeStruct((32, 32), F32),
            jax.ShapeDtypeStruct((1, D), F32),
        ),
        in_specs=[any_space, any_space, vmem, vmem, vmem],
        out_specs=(any_space, vmem, vmem, vmem),
        scratch_shapes=scratch,
        name="dense_back",
        compiler_params=pltpu.CompilerParams(
            collective_id=0, has_side_effects=True, vmem_limit_bytes=56 << 20
        ),
    )(outputs[0], cotangents[0], gain, w_in[0].T, w_out[0])
    return grad[None], gwin.T[None], gwout[None], ggain


def solution(mesh):
    placed = (
        P("section", "dp", None),
        P("section", None, "dp", None),
        P("section", None),
        P("section", None, None),
        P("section", None, None),
    )
    return jax.shard_map(
        shards,
        mesh=mesh,
        in_specs=placed,
        out_specs=(
            P("section", "dp", None),
            P("section", None, None),
            P("section", None, None),
            P("section", None),
        ),
        check_vma=False,
    )
```

```python
import functools

import jax
import jax.numpy as jnp
from jax import lax
from jax.experimental import pallas as pl
from jax.experimental.pallas import tpu as pltpu
from jax.sharding import PartitionSpec as P

ND = 12
NB = 1
PF = 3
PF_TOP = 6
MESH = pl.DeviceIdType.MESH
F32 = jnp.float32
BF16 = jnp.bfloat16
C0 = 0.7978845608028654
C1 = 0.044715


def gelu(v):
    return 0.5 * v * (1.0 + jnp.tanh(C0 * (v + C1 * v * v * v)))


def gelu_slope(v):
    t = jnp.tanh(C0 * (v + C1 * v * v * v))
    return 0.5 * (1.0 + t) + 0.5 * v * (1.0 - t * t) * (C0 * (1.0 + 3.0 * C1 * v * v))


def nt(a, b):
    return lax.dot_general(a, b, (((1,), (1,)), ((), ())), preferred_element_type=F32)


def tn(a, b):
    return lax.dot_general(a, b, (((0,), (0,)), ((), ())), preferred_element_type=F32)


def iota(shape, dim):
    return lax.broadcasted_iota(jnp.int32, shape, dim)


def kernel(
    nq, x_ref, cot_ref, gain_ref, win_ref, wout_ref,
    out_ref, gwin_ref, gwout_ref, ggain_ref,
    X, HN, OUT, GG, G, C, CB, PB, R, SR, PS, A, A3, ACC, ACC3,
    PRE, RI, MS, WF, WS, W3, DMT, DM, DMB, D3X, DP, WO,
    HT, MSG, MR, ZS, ZR, AG,
    x_sem, out_sem, lg_sem, lc_sem, sg_s, sg_r, sc_s, sc_r, up_s, up_r, fw_s, fw_r,
    dn_s, dn_r, cb_s, cb_r, ss_s, ss_r, w_s, w_r, w3_s, w3_r, dm_s, dm_r, d3_s, d3_r,
    ht_s, ht_r, ms_s, ms_r, z_s, z_r, ag_s, ag_r,
):
    D = x_ref.shape[1]
    DC = D // ND
    CW = D // nq
    s = lax.axis_index("section")
    dp = lax.axis_index("dp")
    k = s // 2
    c = s % 2
    q = dp // 2
    zh = dp % 2
    sib = s + 1 - 2 * c
    top = k == 3
    below_top = k < 3

    def half(h):
        return pl.ds(pl.multiple_of(h * 64, 64), 64)

    def cols(d):
        return pl.ds(pl.multiple_of(d * DC, 128), DC)

    def wide(p):
        return pl.ds(pl.multiple_of(p * CW, 128), CW)

    def send(src, dst, ss, rs, to):
        return pltpu.make_async_remote_copy(
            src_ref=src, dst_ref=dst, send_sem=ss, recv_sem=rs, device_id=to, device_id_type=MESH
        )

    def sec(n):
        return {"section": n}

    def load_x():
        return pltpu.make_async_copy(x_ref, X, x_sem)

    def load_g(d):
        return pltpu.make_async_copy(x_ref.at[half(c), cols(d)], G.at[d, s], lg_sem.at[d])

    def load_c(d):
        return pltpu.make_async_copy(
            cot_ref.at[:, half(c), cols(d)], C.at[d, pl.ds(4 * c, 4)], lc_sem.at[d]
        )

    def sib_g(d):
        return send(x_ref.at[half(1 - c), cols(d)], G.at[d, s], sg_s.at[d], sg_r.at[d], sec(sib))

    def sib_c(d):
        return send(
            cot_ref.at[:, half(1 - c), cols(d)], C.at[d, pl.ds(4 * c, 4)], sc_s.at[d], sc_r.at[d], sec(sib)
        )

    def up_own(d, h, source):
        to = jnp.minimum(2 * k + 2 + h, 7)
        return send(x_ref.at[half(h), cols(d)], G.at[d, s], up_s.at[d, h], up_r.at[d, source], sec(to))

    def up_fwd(d, m):
        pair = pl.ds(2 * m, 2)
        return send(
            G.at[d, pair], G.at[d, pair], fw_s.at[d, m], fw_r.at[d, m], sec(jnp.minimum(s + 2, 7))
        )

    def down(d, m):
        pair = pl.ds(2 * m, 2)
        return send(
            PB.at[d, pair], R.at[d, pair], dn_s.at[d, m], dn_r.at[d, m], sec(jnp.maximum(s - 2, 0))
        )

    def hand(d, h, source):
        return send(
            cot_ref.at[:, half(h), cols(d)], CB.at[d, pl.ds(4 * c, 4)], cb_s.at[d, h], cb_r.at[d, source],
            sec(4 + h),
        )

    def sib_s(d):
        return send(PB.at[d, sib], SR.at[d], ss_s.at[d], ss_r.at[d], sec(sib))

    def sib_w():
        return send(WF.at[half(1 - c)], WS.at[c], w_s, w_r, sec(sib))

    def top_w(h, source):
        return send(WF.at[half(h)], W3.at[c], w3_s.at[h], w3_r.at[source], sec(4 + h))

    def sib_dm():
        return send(DMT.at[1 - c], DM.at[c], dm_s, dm_r, sec(sib))

    def top_dm(cc, source):
        return send(D3X.at[cc], DMB.at[c], d3_s.at[cc], d3_r.at[source], sec(6 + cc))

    def peer(p):
        return {"dp": 2 * p + zh}

    def turn(p, source):
        return send(HN.at[:, wide(p)], HT.at[q], ht_s.at[p], ht_r.at[source], peer(p))

    def tell(p, source):
        return send(MSG, MR.at[q], ms_s.at[p], ms_r.at[source], peer(p))

    def swap():
        return send(ZS, ZR, z_s, z_r, {"dp": dp + 1 - 2 * zh})

    def ag(p, source):
        return send(AG.at[q], AG.at[q], ag_s.at[p], ag_r.at[source], peer(p))

    def around(o):
        return lax.rem(q + o, nq)

    load_x().start()

    def first_loads(d, carry):
        load_c(d).start()
        load_g(d).start()
        return carry

    lax.fori_loop(0, PF, first_loads, 0)

    barrier = pltpu.get_barrier_semaphore()

    def greet(to):
        pl.semaphore_signal(barrier, inc=1, device_id=to, device_id_type=MESH)

    greet(sec(sib))
    for h in range(2):

        @pl.when(below_top)
        def _():
            greet(sec(jnp.minimum(2 * k + 2 + h, 7)))

        @pl.when(k > 0)
        def _():
            greet(sec(jnp.maximum(2 * k - 2 + h, 0)))

    def greet_peer(o, carry):
        greet(peer(around(o)))
        return carry

    lax.fori_loop(1, nq, greet_peer, 0)
    greet({"dp": dp + 1 - 2 * zh})
    sides = jnp.where(below_top, 2, 0) + jnp.where(k > 0, 2, 0)
    pl.semaphore_wait(barrier, nq + 1 + sides)

    def goes_up(d):
        return jnp.logical_and(below_top, jnp.logical_or(k < 2, d >= NB))

    def start_up(d):
        @pl.when(goes_up(d))
        def _():
            for h in range(2):
                up_own(d, h, c).start()

    @pl.when(top)
    def _():
        for d in range(NB):
            for h in range(2):
                hand(d, h, c).start()

    def first_sends(d, carry):
        start_up(d)
        sib_c(d).start()
        sib_g(d).start()
        return carry

    lax.fori_loop(0, PF, first_sends, 0)
    ahead = jnp.where(k == 2, PF_TOP, PF)

    def more_up(d, carry):
        start_up(d)
        return carry

    lax.fori_loop(PF, ahead, more_up, 0)

    speed = jnp.where(k < 2, 4, 3)

    def used(i):
        return jnp.minimum(ND, jnp.where(top, i + 1, ((i + 1) * speed) // 2))

    @pl.when(top)
    def _():
        for d in range(NB):
            for j in range(6):
                G[d, j] = jnp.zeros((64, DC), BF16)

    load_x().wait()
    step = D // 6

    def norm_rows(r, carry):
        rows = pl.ds(pl.multiple_of(r * 16, 16), 16)
        total = jnp.zeros((16, 1), F32)
        for p in range(6):
            v = X[rows, p * step : (p + 1) * step].astype(F32)
            total = total + jnp.sum(v * v, axis=1, keepdims=True)
        rinv = lax.rsqrt(total * (1.0 / D) + 1e-06)
        RI[rows, :] = rinv
        for p in range(6):
            at = slice(p * step, (p + 1) * step)
            HN[rows, at] = (X[rows, at].astype(F32) * rinv * gain_ref[:, at]).astype(BF16)
        return carry

    lax.fori_loop(0, 8, norm_rows, 0)
    pre = nt(win_ref[...], HN[...])
    PRE[...] = pre
    mixw = tn(gelu(pre).astype(BF16), wout_ref[...])
    mixw = jnp.where((iota((128, 32), 1) & 7) <= s, mixw, 0.0)
    WF[...] = jnp.zeros((128, 128), BF16)
    WF[:, 0:32] = mixw.astype(BF16)
    sib_w().start()

    @pl.when(top)
    def _():
        for h in range(2):
            top_w(h, c).start()

    WS[c] = WF[half(c), :]
    for g in range(2):
        ACC[g] = jnp.zeros((256, 256), F32)
    sib_w().wait_recv()

    def spread(W, A):
        row = iota((256, 128), 0)
        lane = iota((256, 128), 1)
        pick = jnp.logical_and(lane < 32, (lane & 7) == (row >> 5))
        srow = iota((128, 256), 0)
        scol = iota((128, 256), 1)
        same = (iota((256, 256), 0) & 31) == (iota((256, 256), 1) & 31)
        for g in range(2):
            total = jnp.zeros((256, 256), F32)
            for cc in range(2):
                w = W[cc, 32 * g : 32 * g + 32, :].astype(F32)
                w = jnp.where(pick, jnp.concatenate([w] * 8, axis=0), 0.0).astype(BF16)
                place = jnp.logical_and(srow < 32, (scol >> 5) == 4 * cc + (srow >> 3))
                total = total + jnp.dot(w, jnp.where(place, 1.0, 0.0).astype(BF16), preferred_element_type=F32)
            A[g] = jnp.where(same, total, 0.0).astype(BF16)

    spread(WS, A)
    HT[q] = HN[:, wide(q)]

    def start_turn(o, carry):
        turn(around(o), q).start()
        return carry

    lax.fori_loop(1, nq, start_turn, 0)

    def group(ref, d, g):
        return ref[d, :, 32 * g : 32 * g + 32, :].reshape(256, DC)

    def stage_part(d):
        handed = d < NB

        @pl.when(top)
        def _():
            load_c(d).wait()
            sib_c(d).wait_recv()

        for g in range(2):
            PS[g] = jnp.dot(A[g], group(C, d, g), preferred_element_type=F32)

        @pl.when(jnp.logical_and(k == 2, handed))
        def _():
            for a in range(2):
                hand(d, 0, a).wait_recv()
            for g in range(2):
                PS[g] = PS[g] + jnp.dot(A3[g], group(CB, d, g), preferred_element_type=F32)
                ACC3[g] = ACC3[g] + nt(group(CB, d, g), group(G, d, g))

        takes = jnp.logical_and(below_top, jnp.logical_or(k < 2, d >= NB))
        for m in range(4):

            def keep(with_r):
                for g in range(2):
                    rows = slice(32 * g, 32 * g + 32)
                    own = PS[g, 64 * m : 64 * m + 64, :].reshape(2, 32, DC)
                    if with_r:
                        own = own + R[d, 2 * m : 2 * m + 2, rows, :].astype(F32)
                    PB[d, 2 * m : 2 * m + 2, rows, :] = own.astype(BF16)

            if m < 3:

                @pl.when(jnp.logical_and(m <= k, takes))
                def _():
                    down(d, m).wait_recv()
                    keep(True)

            @pl.when(jnp.logical_and(m <= k, jnp.logical_not(takes)))
            def _():
                keep(False)

            if m < 3:

                @pl.when(jnp.logical_and(m < k, jnp.logical_or(below_top, d >= NB)))
                def _():
                    down(d, m).start()

            @pl.when(m == k)
            def _():
                sib_s(d).start()

    def stage_gather(d):
        for m in (2, 1, 0):

            @pl.when(jnp.logical_and(m < k, jnp.logical_or(below_top, d >= NB)))
            def _():
                @pl.when(m == k - 1)
                def _():
                    for a in range(2):
                        up_own(d, 0, a).wait_recv()

                if m < 2:

                    @pl.when(m < k - 1)
                    def _():
                        up_fwd(d, m).wait_recv()

                    @pl.when(goes_up(d))
                    def _():
                        up_fwd(d, m).start()

    def stage_dmix(d):
        @pl.when(below_top)
        def _():
            load_c(d).wait()
            sib_c(d).wait_recv()

        load_g(d).wait()
        sib_g(d).wait_recv()
        for g in range(2):
            ACC[g] = ACC[g] + nt(group(C, d, g), group(G, d, g))

    def extract(acc, low, rise, into):
        row = iota((256, 256), 0)
        col = iota((256, 256), 1)
        ok = jnp.logical_and((row & 31) == (col & 31), (col >> 5) <= low + rise * (row >> 7))
        srow = iota((256, 128), 0)
        lane = iota((256, 128), 1)
        place = jnp.where(jnp.logical_and(lane < 32, (lane & 7) == (srow >> 5)), 1.0, 0.0)
        mine = (lane >> 3) == ((srow >> 5) & 3)
        for g in range(2):
            v = jnp.where(ok, acc[g], 0.0)
            v = jnp.dot(v, place, precision=lax.Precision.HIGHEST, preferred_element_type=F32)
            v = jnp.where(mine, v, 0.0)
            for cc in range(2):
                into[cc, 32 * g : 32 * g + 32, :] = sum(
                    v[128 * cc + 32 * st : 128 * cc + 32 * st + 32] for st in range(4)
                )

    def stage_grads():
        extract(ACC, 2 * k, 1, DMT)
        sib_dm().start()
        DM[c] = DMT[c]
        sib_dm().wait_recv()

        @pl.when(top)
        def _():
            for a in range(2):
                top_dm(0, a).wait_recv()
            DM[...] = DM[...] + DMB[...]

        dflat = DM[...].reshape(128, 128)[:, 0:32].astype(BF16)
        pre = PRE[...]
        dpre = (gelu_slope(pre) * nt(wout_ref[...], dflat)).astype(BF16)
        DP[...] = dpre
        wgrad = jnp.dot(gelu(pre).astype(BF16), dflat, preferred_element_type=F32)
        MSG[0:32, :] = dpre
        MSG[32:48, :] = jnp.zeros((16, 128), BF16)
        MSG[32:48, 0:32] = wgrad[0:16].astype(BF16)
        MSG[32:48, 32:64] = wgrad[16:32].astype(BF16)
        MR[q] = MSG[...]

        def give(o, carry):
            tell(around(o), q).start()
            return carry

        lax.fori_loop(1, nq, give, 0)
        along = lax.dot_general(
            pre * dpre.astype(F32), jnp.ones((32, 128), F32), (((0,), (0,)), ((), ())),
            precision=lax.Precision.HIGHEST, preferred_element_type=F32,
        )
        MS[...] = along[:, 0:1] * (1.0 / D)
        gates(0, part)

    part = nq // 3

    def gates(lo, hi):
        def gate(p, carry):
            at = wide(p)
            dn = tn(DP[...], win_ref[:, at]) * gain_ref[:, at]
            normed = X[:, at].astype(F32) * RI[...]
            GG[:, at] = RI[...] * (dn - normed * MS[...])
            return carry

        lax.fori_loop(lo, hi, gate, 0)

    def stage_sum():
        def hear(o, carry):
            p = around(o)
            turn(0, p).wait_recv()
            tell(0, p).wait_recv()
            return carry

        lax.fori_loop(1, nq, hear, 0)
        told = jnp.concatenate([MR[p, 0:32, :] for p in range(nq)], axis=1)
        ZS[0:32, :] = jnp.dot(told, HT[...].reshape(nq * 128, CW), preferred_element_type=F32).astype(BF16)
        wgrad = sum(MR[p, 32:48, :].astype(F32) for p in range(nq))
        ZS[32:48, :] = jnp.zeros((16, CW), BF16)
        ZS[32:48, 0:128] = wgrad.astype(BF16)
        swap().start()
        gates(part, 2 * part)

    def stage_share():
        swap().wait_recv()
        both = ZS[...].astype(F32) + ZR[...].astype(F32)
        AG[q] = both[0:32].astype(BF16)

        def give(o, carry):
            ag(around(o), q).start()
            return carry

        lax.fori_loop(1, nq, give, 0)
        WO[...] = both[32:48, 0:128]
        gates(2 * part, nq)

    def finish(d, carry):
        sib_s(d).wait_recv()
        at = cols(d)
        OUT[half(c), at] = (PB[d, s].astype(F32) + GG[half(c), at]).astype(BF16)
        OUT[half(1 - c), at] = (SR[d].astype(F32) + GG[half(1 - c), at]).astype(BF16)
        return carry

    early = 3 * ND // 4

    def store(e):
        at = slice(0, early * DC) if e == 0 else slice(early * DC, D)
        return pltpu.make_async_copy(OUT.at[:, at], out_ref.at[:, at], out_sem.at[e])

    def stage_finish():
        lax.fori_loop(0, early, finish, 0)
        store(0).start()

    @pl.when(k == 2)
    def _():
        for a in range(2):
            top_w(0, a).wait_recv()
        spread(W3, A3)
        for g in range(2):
            ACC3[g] = jnp.zeros((256, 256), F32)

    lead_part = jnp.where(top, 0, 1)
    tail = jnp.where(top, 2 * ND, (2 * ND + 2) // 3)

    def body(i, carry):
        def loads(d, carry):
            load_c(d).start()
            load_g(d).start()
            sib_c(d).start()
            sib_g(d).start()
            return carry

        lax.fori_loop(jnp.minimum(ND, used(i - 1) + PF), jnp.minimum(ND, used(i) + PF), loads, 0)
        lax.fori_loop(jnp.minimum(ND, used(i - 1) + ahead), jnp.minimum(ND, used(i) + ahead), more_up, 0)

        @pl.when(jnp.logical_and(k == 2, i == NB + 1))
        def _():
            extract(ACC3, 5, 0, D3X)
            for cc in range(2):
                top_dm(cc, c).start()

        pl.when(i == tail)(stage_grads)
        pl.when(i == tail + 1)(stage_sum)
        pl.when(i == tail + 2)(stage_share)
        pl.when(i == tail + 3)(stage_finish)
        d = i - lead_part

        @pl.when(jnp.logical_and(d >= 0, d < ND))
        def _():
            stage_part(d)

        def dots(d, carry):
            stage_gather(d)
            stage_dmix(d)
            return carry

        lo = jnp.where(top, jnp.clip(i - ND, 0, ND), used(i - 1))
        hi = jnp.where(top, jnp.clip(i - ND + 1, 0, ND), used(i))
        lax.fori_loop(lo, hi, dots, 0)
        return carry

    lax.fori_loop(0, 2 * ND + 4, body, 0)

    lax.fori_loop(early, ND, finish, 0)
    store(1).start()

    def unpack(o, carry):
        p = around(o)

        @pl.when(o < nq)
        def _():
            ag(0, p).wait_recv()

        at = wide(p)
        m = AG[p].astype(F32)
        gwin_ref[:, at] = m
        ggain_ref[:, at] = jnp.sum(m * win_ref[:, at].astype(F32), axis=0, keepdims=True) / gain_ref[:, at]
        return carry

    lax.fori_loop(1, nq + 1, unpack, 0)
    gwout_ref[0:16, :] = WO[:, 0:32]
    gwout_ref[16:32, :] = WO[:, 32:64]

    def drain(d, carry):
        sib_c(d).wait_send()
        sib_g(d).wait_send()
        sib_s(d).wait_send()

        @pl.when(goes_up(d))
        def _():
            for h in range(2):
                up_own(d, h, c).wait_send()
            for m in range(2):

                @pl.when(m < k)
                def _():
                    up_fwd(d, m).wait_send()

        for m in range(3):

            @pl.when(jnp.logical_and(m < k, jnp.logical_or(below_top, d >= NB)))
            def _():
                down(d, m).wait_send()

        return carry

    lax.fori_loop(0, ND, drain, 0)
    sib_w().wait_send()
    sib_dm().wait_send()

    @pl.when(top)
    def _():
        for h in range(2):
            top_w(h, c).wait_send()
            for d in range(NB):
                hand(d, h, c).wait_send()

    @pl.when(k == 2)
    def _():
        for cc in range(2):
            top_dm(cc, c).wait_send()

    def drain_peer(o, carry):
        p = around(o)
        turn(p, q).wait_send()
        tell(p, q).wait_send()
        ag(p, q).wait_send()
        return carry

    lax.fori_loop(1, nq, drain_peer, 0)
    swap().wait_send()
    for e in range(2):
        store(e).wait()


def copies(g_ref, w_ref, o_ref, n_ref, g_out, w_out, o_out, n_out, G, W, O, N, read, write):
    rows = G.shape[0] // 4
    pairs = [(g_ref.at[pl.ds(e * rows, rows)], G.at[pl.ds(e * rows, rows)], g_out.at[pl.ds(e * rows, rows)]) for e in range(4)]
    rows_w = W.shape[0] // 2
    pairs += [(w_ref.at[pl.ds(e * rows_w, rows_w)], W.at[pl.ds(e * rows_w, rows_w)], w_out.at[pl.ds(e * rows_w, rows_w)]) for e in range(2)]
    pairs += [(o_ref, O, o_out), (n_ref, N, n_out)]
    reads = [pltpu.make_async_copy(a, b, read.at[i]) for i, (a, b, _) in enumerate(pairs)]
    writes = [pltpu.make_async_copy(b, c, write.at[i]) for i, (_, b, c) in enumerate(pairs)]
    for move in reads:
        move.start()
    for i in range(len(pairs)):
        reads[i].wait()
        writes[i].start()
    for move in writes:
        move.wait()


def hand_over(*arrays):
    any_space = pl.BlockSpec(memory_space=pl.ANY)
    return pl.pallas_call(
        copies,
        out_shape=tuple(jax.ShapeDtypeStruct(a.shape, a.dtype) for a in arrays),
        in_specs=[any_space] * len(arrays),
        out_specs=(any_space,) * len(arrays),
        scratch_shapes=[pltpu.VMEM(a.shape, a.dtype) for a in arrays] + [pltpu.SemaphoreType.DMA((8,))] * 2,
        name="hand_over",
        compiler_params=pltpu.CompilerParams(vmem_limit_bytes=56 << 20),
    )(*arrays)


def shards(outputs, cotangents, gain, w_in, w_out):
    D = outputs.shape[2]
    nq = lax.axis_size("dp") // 2
    DC = D // ND
    CW = D // nq
    dma = pltpu.SemaphoreType.DMA
    any_space = pl.BlockSpec(memory_space=pl.ANY)
    vmem = pl.BlockSpec(memory_space=pltpu.VMEM)
    scratch = [
        pltpu.VMEM((128, D), BF16),
        pltpu.VMEM((128, D), BF16),
        pltpu.VMEM((128, D), BF16),
        pltpu.VMEM((128, D), F32),
        pltpu.VMEM((ND, 8, 64, DC), BF16),
        pltpu.VMEM((ND, 8, 64, DC), BF16),
        pltpu.VMEM((NB, 8, 64, DC), BF16),
        pltpu.VMEM((ND, 8, 64, DC), BF16),
        pltpu.VMEM((ND, 6, 64, DC), BF16),
        pltpu.VMEM((ND, 64, DC), BF16),
        pltpu.VMEM((2, 256, DC), F32),
        pltpu.VMEM((2, 256, 256), BF16),
        pltpu.VMEM((2, 256, 256), BF16),
        pltpu.VMEM((2, 256, 256), F32),
        pltpu.VMEM((2, 256, 256), F32),
        pltpu.VMEM((32, 128), F32),
        pltpu.VMEM((128, 1), F32),
        pltpu.VMEM((128, 1), F32),
        pltpu.VMEM((128, 128), BF16),
        pltpu.VMEM((2, 64, 128), BF16),
        pltpu.VMEM((2, 64, 128), BF16),
        pltpu.VMEM((2, 64, 128), F32),
        pltpu.VMEM((2, 64, 128), F32),
        pltpu.VMEM((2, 64, 128), F32),
        pltpu.VMEM((2, 64, 128), F32),
        pltpu.VMEM((32, 128), BF16),
        pltpu.VMEM((16, 128), F32),
        pltpu.VMEM((nq, 128, CW), BF16),
        pltpu.VMEM((48, 128), BF16),
        pltpu.VMEM((nq, 48, 128), BF16),
        pltpu.VMEM((48, CW), BF16),
        pltpu.VMEM((48, CW), BF16),
        pltpu.VMEM((nq, 32, CW), BF16),
        dma, dma((2,)), dma((ND,)), dma((ND,)),
        dma((ND,)), dma((ND,)), dma((ND,)), dma((ND,)),
        dma((ND, 2)), dma((ND, 2)), dma((ND, 2)), dma((ND, 2)),
        dma((ND, 3)), dma((ND, 3)), dma((NB, 2)), dma((NB, 2)),
        dma((ND,)), dma((ND,)), dma, dma, dma((2,)), dma((2,)),
        dma, dma, dma((2,)), dma((2,)),
        dma((nq,)), dma((nq,)), dma((nq,)), dma((nq,)),
        dma, dma, dma((nq,)), dma((nq,)),
    ]
    grad, gwin, gwout, ggain = pl.pallas_call(
        functools.partial(kernel, nq),
        out_shape=(
            jax.ShapeDtypeStruct((128, D), BF16),
            jax.ShapeDtypeStruct((32, D), F32),
            jax.ShapeDtypeStruct((32, 32), F32),
            jax.ShapeDtypeStruct((1, D), F32),
        ),
        in_specs=[any_space, any_space, vmem, vmem, vmem],
        out_specs=(any_space, vmem, vmem, vmem),
        scratch_shapes=scratch,
        name="dense_back",
        compiler_params=pltpu.CompilerParams(
            collective_id=0, has_side_effects=True, vmem_limit_bytes=56 << 20
        ),
    )(outputs[0], cotangents[0], gain, w_in[0].T, w_out[0])
    grad, gwin, gwout, ggain = hand_over(grad, gwin, gwout, ggain)
    return grad[None], gwin.T[None], gwout[None], ggain


def solution(mesh):
    placed = (
        P("section", "dp", None),
        P("section", None, "dp", None),
        P("section", None),
        P("section", None, None),
        P("section", None, None),
    )
    return jax.shard_map(
        shards,
        mesh=mesh,
        in_specs=placed,
        out_specs=(
            P("section", "dp", None),
            P("section", None, None),
            P("section", None, None),
            P("section", None),
        ),
        check_vma=False,
    )
```

```python
import functools

import jax
import jax.numpy as jnp
from jax import lax
from jax.experimental import pallas as pl
from jax.experimental.pallas import tpu as pltpu
from jax.sharding import PartitionSpec as P

ND = 8
NB = 1
PF = 3
PF_TOP = 6
MESH = pl.DeviceIdType.MESH
F32 = jnp.float32
BF16 = jnp.bfloat16
C0 = 0.7978845608028654
C1 = 0.044715


def gelu(v):
    return 0.5 * v * (1.0 + jnp.tanh(C0 * (v + C1 * v * v * v)))


def gelu_slope(v):
    t = jnp.tanh(C0 * (v + C1 * v * v * v))
    return 0.5 * (1.0 + t) + 0.5 * v * (1.0 - t * t) * (C0 * (1.0 + 3.0 * C1 * v * v))


def nt(a, b):
    return lax.dot_general(a, b, (((1,), (1,)), ((), ())), preferred_element_type=F32)


def tn(a, b):
    return lax.dot_general(a, b, (((0,), (0,)), ((), ())), preferred_element_type=F32)


def iota(shape, dim):
    return lax.broadcasted_iota(jnp.int32, shape, dim)


def kernel(
    nq, x_ref, cot_ref, gain_ref, win_ref, wout_ref,
    out_ref, gwin_ref, gwout_ref, ggain_ref,
    X, HN, OUT, GG, G, C, CB, PB, R, SR, PS, A, A3, ACC, ACC3,
    PRE, RI, MS, WF, WS, W3, DMT, DM, DMB, D3X, DP, WO,
    HT, MSG, MR, ZS, ZR, AG,
    x_sem, out_sem, lg_sem, lc_sem, sg_s, sg_r, sc_s, sc_r, up_s, up_r, fw_s, fw_r,
    dn_s, dn_r, cb_s, cb_r, ss_s, ss_r, w_s, w_r, w3_s, w3_r, dm_s, dm_r, d3_s, d3_r,
    ht_s, ht_r, ms_s, ms_r, z_s, z_r, ag_s, ag_r,
):
    D = x_ref.shape[1]
    DC = D // ND
    CW = D // nq
    s = lax.axis_index("section")
    dp = lax.axis_index("dp")
    k = s // 2
    c = s % 2
    q = dp // 2
    zh = dp % 2
    sib = s + 1 - 2 * c
    top = k == 3
    below_top = k < 3

    def half(h):
        return pl.ds(pl.multiple_of(h * 64, 64), 64)

    def cols(d):
        return pl.ds(pl.multiple_of(d * DC, 128), DC)

    def wide(p):
        return pl.ds(pl.multiple_of(p * CW, 128), CW)

    def send(src, dst, ss, rs, to):
        return pltpu.make_async_remote_copy(
            src_ref=src, dst_ref=dst, send_sem=ss, recv_sem=rs, device_id=to, device_id_type=MESH
        )

    def sec(n):
        return {"section": n}

    def load_x():
        return pltpu.make_async_copy(x_ref, X, x_sem)

    def load_g(d):
        return pltpu.make_async_copy(x_ref.at[half(c), cols(d)], G.at[d, s], lg_sem.at[d])

    def load_c(d):
        return pltpu.make_async_copy(
            cot_ref.at[:, half(c), cols(d)], C.at[d, pl.ds(4 * c, 4)], lc_sem.at[d]
        )

    def sib_g(d):
        return send(x_ref.at[half(1 - c), cols(d)], G.at[d, s], sg_s.at[d], sg_r.at[d], sec(sib))

    def sib_c(d):
        return send(
            cot_ref.at[:, half(1 - c), cols(d)], C.at[d, pl.ds(4 * c, 4)], sc_s.at[d], sc_r.at[d], sec(sib)
        )

    def up_own(d, h, source):
        to = jnp.minimum(2 * k + 2 + h, 7)
        return send(x_ref.at[half(h), cols(d)], G.at[d, s], up_s.at[d, h], up_r.at[d, source], sec(to))

    def up_fwd(d, m):
        pair = pl.ds(2 * m, 2)
        return send(
            G.at[d, pair], G.at[d, pair], fw_s.at[d, m], fw_r.at[d, m], sec(jnp.minimum(s + 2, 7))
        )

    def down(d, m):
        pair = pl.ds(2 * m, 2)
        return send(
            PB.at[d, pair], R.at[d, pair], dn_s.at[d, m], dn_r.at[d, m], sec(jnp.maximum(s - 2, 0))
        )

    def hand(d, h, source):
        return send(
            cot_ref.at[:, half(h), cols(d)], CB.at[d, pl.ds(4 * c, 4)], cb_s.at[d, h], cb_r.at[d, source],
            sec(4 + h),
        )

    def sib_s(d):
        return send(PB.at[d, sib], SR.at[d], ss_s.at[d], ss_r.at[d], sec(sib))

    def sib_w():
        return send(WF.at[half(1 - c)], WS.at[c], w_s, w_r, sec(sib))

    def top_w(h, source):
        return send(WF.at[half(h)], W3.at[c], w3_s.at[h], w3_r.at[source], sec(4 + h))

    def sib_dm():
        return send(DMT.at[1 - c], DM.at[c], dm_s, dm_r, sec(sib))

    def top_dm(cc, source):
        return send(D3X.at[cc], DMB.at[c], d3_s.at[cc], d3_r.at[source], sec(6 + cc))

    def peer(p):
        return {"dp": 2 * p + zh}

    def turn(p, source):
        return send(HN.at[:, wide(p)], HT.at[q], ht_s.at[p], ht_r.at[source], peer(p))

    def tell(p, source):
        return send(MSG, MR.at[q], ms_s.at[p], ms_r.at[source], peer(p))

    def swap():
        return send(ZS, ZR, z_s, z_r, {"dp": dp + 1 - 2 * zh})

    def ag(p, source):
        return send(AG.at[q], AG.at[q], ag_s.at[p], ag_r.at[source], peer(p))

    def around(o):
        return lax.rem(q + o, nq)

    load_x().start()

    def first_loads(d, carry):
        load_c(d).start()
        load_g(d).start()
        return carry

    lax.fori_loop(0, PF, first_loads, 0)

    barrier = pltpu.get_barrier_semaphore()

    def greet(to):
        pl.semaphore_signal(barrier, inc=1, device_id=to, device_id_type=MESH)

    greet(sec(sib))
    for h in range(2):

        @pl.when(below_top)
        def _():
            greet(sec(jnp.minimum(2 * k + 2 + h, 7)))

        @pl.when(k > 0)
        def _():
            greet(sec(jnp.maximum(2 * k - 2 + h, 0)))

    def greet_peer(o, carry):
        greet(peer(around(o)))
        return carry

    lax.fori_loop(1, nq, greet_peer, 0)
    greet({"dp": dp + 1 - 2 * zh})
    sides = jnp.where(below_top, 2, 0) + jnp.where(k > 0, 2, 0)
    pl.semaphore_wait(barrier, nq + 1 + sides)

    def goes_up(d):
        return jnp.logical_and(below_top, jnp.logical_or(k < 2, d >= NB))

    def start_up(d):
        @pl.when(goes_up(d))
        def _():
            for h in range(2):
                up_own(d, h, c).start()

    @pl.when(top)
    def _():
        for d in range(NB):
            for h in range(2):
                hand(d, h, c).start()

    def first_sends(d, carry):
        start_up(d)
        sib_c(d).start()
        sib_g(d).start()
        return carry

    lax.fori_loop(0, PF, first_sends, 0)
    ahead = jnp.where(k == 2, PF_TOP, PF)

    def more_up(d, carry):
        start_up(d)
        return carry

    lax.fori_loop(PF, ahead, more_up, 0)

    speed = jnp.where(k < 2, 4, 3)

    def used(i):
        return jnp.minimum(ND, jnp.where(top, i + 1, ((i + 1) * speed) // 2))

    @pl.when(top)
    def _():
        for d in range(NB):
            for j in range(6):
                G[d, j] = jnp.zeros((64, DC), BF16)

    load_x().wait()
    step = D // 6

    def norm_rows(r, carry):
        rows = pl.ds(pl.multiple_of(r * 16, 16), 16)
        total = jnp.zeros((16, 1), F32)
        for p in range(6):
            v = X[rows, p * step : (p + 1) * step].astype(F32)
            total = total + jnp.sum(v * v, axis=1, keepdims=True)
        rinv = lax.rsqrt(total * (1.0 / D) + 1e-06)
        RI[rows, :] = rinv
        for p in range(6):
            at = slice(p * step, (p + 1) * step)
            HN[rows, at] = (X[rows, at].astype(F32) * rinv * gain_ref[:, at]).astype(BF16)
        return carry

    lax.fori_loop(0, 8, norm_rows, 0)
    pre = nt(win_ref[...], HN[...])
    PRE[...] = pre
    mixw = tn(gelu(pre).astype(BF16), wout_ref[...])
    mixw = jnp.where((iota((128, 32), 1) & 7) <= s, mixw, 0.0)
    WF[...] = jnp.zeros((128, 128), BF16)
    WF[:, 0:32] = mixw.astype(BF16)
    sib_w().start()

    @pl.when(top)
    def _():
        for h in range(2):
            top_w(h, c).start()

    WS[c] = WF[half(c), :]
    for g in range(2):
        ACC[g] = jnp.zeros((256, 256), F32)
    sib_w().wait_recv()

    def spread(W, A):
        row = iota((256, 128), 0)
        lane = iota((256, 128), 1)
        pick = jnp.logical_and(lane < 32, (lane & 7) == (row >> 5))
        srow = iota((128, 256), 0)
        scol = iota((128, 256), 1)
        same = (iota((256, 256), 0) & 31) == (iota((256, 256), 1) & 31)
        for g in range(2):
            total = jnp.zeros((256, 256), F32)
            for cc in range(2):
                w = W[cc, 32 * g : 32 * g + 32, :].astype(F32)
                w = jnp.where(pick, jnp.concatenate([w] * 8, axis=0), 0.0).astype(BF16)
                place = jnp.logical_and(srow < 32, (scol >> 5) == 4 * cc + (srow >> 3))
                total = total + jnp.dot(w, jnp.where(place, 1.0, 0.0).astype(BF16), preferred_element_type=F32)
            A[g] = jnp.where(same, total, 0.0).astype(BF16)

    spread(WS, A)
    HT[q] = HN[:, wide(q)]

    def start_turn(o, carry):
        turn(around(o), q).start()
        return carry

    lax.fori_loop(1, nq, start_turn, 0)

    def group(ref, d, g):
        return ref[d, :, 32 * g : 32 * g + 32, :].reshape(256, DC)

    def stage_part(d):
        handed = d < NB

        @pl.when(top)
        def _():
            load_c(d).wait()
            sib_c(d).wait_recv()

        for g in range(2):
            PS[g] = jnp.dot(A[g], group(C, d, g), preferred_element_type=F32)

        @pl.when(jnp.logical_and(k == 2, handed))
        def _():
            for a in range(2):
                hand(d, 0, a).wait_recv()
            for g in range(2):
                PS[g] = PS[g] + jnp.dot(A3[g], group(CB, d, g), preferred_element_type=F32)
                ACC3[g] = ACC3[g] + nt(group(CB, d, g), group(G, d, g))

        takes = jnp.logical_and(below_top, jnp.logical_or(k < 2, d >= NB))
        for m in range(4):

            def keep(with_r):
                for g in range(2):
                    rows = slice(32 * g, 32 * g + 32)
                    own = PS[g, 64 * m : 64 * m + 64, :].reshape(2, 32, DC)
                    if with_r:
                        own = own + R[d, 2 * m : 2 * m + 2, rows, :].astype(F32)
                    PB[d, 2 * m : 2 * m + 2, rows, :] = own.astype(BF16)

            if m < 3:

                @pl.when(jnp.logical_and(m <= k, takes))
                def _():
                    down(d, m).wait_recv()
                    keep(True)

            @pl.when(jnp.logical_and(m <= k, jnp.logical_not(takes)))
            def _():
                keep(False)

            if m < 3:

                @pl.when(jnp.logical_and(m < k, jnp.logical_or(below_top, d >= NB)))
                def _():
                    down(d, m).start()

            @pl.when(m == k)
            def _():
                sib_s(d).start()

    def stage_gather(d):
        for m in (2, 1, 0):

            @pl.when(jnp.logical_and(m < k, jnp.logical_or(below_top, d >= NB)))
            def _():
                @pl.when(m == k - 1)
                def _():
                    for a in range(2):
                        up_own(d, 0, a).wait_recv()

                if m < 2:

                    @pl.when(m < k - 1)
                    def _():
                        up_fwd(d, m).wait_recv()

                    @pl.when(goes_up(d))
                    def _():
                        up_fwd(d, m).start()

    def stage_dmix(d):
        @pl.when(below_top)
        def _():
            load_c(d).wait()
            sib_c(d).wait_recv()

        load_g(d).wait()
        sib_g(d).wait_recv()
        for g in range(2):
            ACC[g] = ACC[g] + nt(group(C, d, g), group(G, d, g))

    def extract(acc, low, rise, into):
        row = iota((256, 256), 0)
        col = iota((256, 256), 1)
        ok = jnp.logical_and((row & 31) == (col & 31), (col >> 5) <= low + rise * (row >> 7))
        srow = iota((256, 128), 0)
        lane = iota((256, 128), 1)
        place = jnp.where(jnp.logical_and(lane < 32, (lane & 7) == (srow >> 5)), 1.0, 0.0)
        mine = (lane >> 3) == ((srow >> 5) & 3)
        for g in range(2):
            v = jnp.where(ok, acc[g], 0.0)
            v = jnp.dot(v, place, precision=lax.Precision.HIGHEST, preferred_element_type=F32)
            v = jnp.where(mine, v, 0.0)
            for cc in range(2):
                into[cc, 32 * g : 32 * g + 32, :] = sum(
                    v[128 * cc + 32 * st : 128 * cc + 32 * st + 32] for st in range(4)
                )

    def stage_grads():
        extract(ACC, 2 * k, 1, DMT)
        sib_dm().start()
        DM[c] = DMT[c]
        sib_dm().wait_recv()

        @pl.when(top)
        def _():
            for a in range(2):
                top_dm(0, a).wait_recv()
            DM[...] = DM[...] + DMB[...]

        dflat = DM[...].reshape(128, 128)[:, 0:32].astype(BF16)
        pre = PRE[...]
        dpre = (gelu_slope(pre) * nt(wout_ref[...], dflat)).astype(BF16)
        DP[...] = dpre
        wgrad = jnp.dot(gelu(pre).astype(BF16), dflat, preferred_element_type=F32)
        MSG[0:32, :] = dpre
        MSG[32:48, :] = jnp.zeros((16, 128), BF16)
        MSG[32:48, 0:32] = wgrad[0:16].astype(BF16)
        MSG[32:48, 32:64] = wgrad[16:32].astype(BF16)
        MR[q] = MSG[...]

        def give(o, carry):
            tell(around(o), q).start()
            return carry

        lax.fori_loop(1, nq, give, 0)
        along = lax.dot_general(
            pre * dpre.astype(F32), jnp.ones((32, 128), F32), (((0,), (0,)), ((), ())),
            precision=lax.Precision.HIGHEST, preferred_element_type=F32,
        )
        MS[...] = along[:, 0:1] * (1.0 / D)
        gates(0, part)

    part = nq // 3

    def gates(lo, hi):
        def gate(p, carry):
            at = wide(p)
            dn = tn(DP[...], win_ref[:, at]) * gain_ref[:, at]
            normed = X[:, at].astype(F32) * RI[...]
            GG[:, at] = RI[...] * (dn - normed * MS[...])
            return carry

        lax.fori_loop(lo, hi, gate, 0)

    def stage_sum():
        def hear(o, carry):
            p = around(o)
            turn(0, p).wait_recv()
            tell(0, p).wait_recv()
            return carry

        lax.fori_loop(1, nq, hear, 0)
        told = jnp.concatenate([MR[p, 0:32, :] for p in range(nq)], axis=1)
        ZS[0:32, :] = jnp.dot(told, HT[...].reshape(nq * 128, CW), preferred_element_type=F32).astype(BF16)
        wgrad = sum(MR[p, 32:48, :].astype(F32) for p in range(nq))
        ZS[32:48, :] = jnp.zeros((16, CW), BF16)
        ZS[32:48, 0:128] = wgrad.astype(BF16)
        swap().start()
        gates(part, 2 * part)

    def stage_share():
        swap().wait_recv()
        both = ZS[...].astype(F32) + ZR[...].astype(F32)
        AG[q] = both[0:32].astype(BF16)

        def give(o, carry):
            ag(around(o), q).start()
            return carry

        lax.fori_loop(1, nq, give, 0)
        WO[...] = both[32:48, 0:128]
        gates(2 * part, nq)

    def finish(d, carry):
        sib_s(d).wait_recv()
        at = cols(d)
        OUT[half(c), at] = (PB[d, s].astype(F32) + GG[half(c), at]).astype(BF16)
        OUT[half(1 - c), at] = (SR[d].astype(F32) + GG[half(1 - c), at]).astype(BF16)
        return carry

    early = 3 * ND // 4

    def store(e):
        at = slice(0, early * DC) if e == 0 else slice(early * DC, D)
        return pltpu.make_async_copy(OUT.at[:, at], out_ref.at[:, at], out_sem.at[e])

    def stage_finish():
        lax.fori_loop(0, early, finish, 0)
        store(0).start()

    @pl.when(k == 2)
    def _():
        for a in range(2):
            top_w(0, a).wait_recv()
        spread(W3, A3)
        for g in range(2):
            ACC3[g] = jnp.zeros((256, 256), F32)

    lead_part = jnp.where(top, 0, 1)
    tail = jnp.where(top, 2 * ND, (2 * ND + 2) // 3)

    def body(i, carry):
        def loads(d, carry):
            load_c(d).start()
            load_g(d).start()
            sib_c(d).start()
            sib_g(d).start()
            return carry

        lax.fori_loop(jnp.minimum(ND, used(i - 1) + PF), jnp.minimum(ND, used(i) + PF), loads, 0)
        lax.fori_loop(jnp.minimum(ND, used(i - 1) + ahead), jnp.minimum(ND, used(i) + ahead), more_up, 0)

        @pl.when(jnp.logical_and(k == 2, i == NB + 1))
        def _():
            extract(ACC3, 5, 0, D3X)
            for cc in range(2):
                top_dm(cc, c).start()

        pl.when(i == tail)(stage_grads)
        pl.when(i == tail + 1)(stage_sum)
        pl.when(i == tail + 2)(stage_share)
        pl.when(i == tail + 3)(stage_finish)
        d = i - lead_part

        @pl.when(jnp.logical_and(d >= 0, d < ND))
        def _():
            stage_part(d)

        def dots(d, carry):
            stage_gather(d)
            stage_dmix(d)
            return carry

        lo = jnp.where(top, jnp.clip(i - ND, 0, ND), used(i - 1))
        hi = jnp.where(top, jnp.clip(i - ND + 1, 0, ND), used(i))
        lax.fori_loop(lo, hi, dots, 0)
        return carry

    lax.fori_loop(0, 2 * ND + 4, body, 0)

    lax.fori_loop(early, ND, finish, 0)
    store(1).start()

    def unpack(o, carry):
        p = around(o)

        @pl.when(o < nq)
        def _():
            ag(0, p).wait_recv()

        at = wide(p)
        m = AG[p].astype(F32)
        gwin_ref[:, at] = m
        ggain_ref[:, at] = jnp.sum(m * win_ref[:, at].astype(F32), axis=0, keepdims=True) / gain_ref[:, at]
        return carry

    lax.fori_loop(1, nq + 1, unpack, 0)
    gwout_ref[0:16, :] = WO[:, 0:32]
    gwout_ref[16:32, :] = WO[:, 32:64]

    def drain(d, carry):
        sib_c(d).wait_send()
        sib_g(d).wait_send()
        sib_s(d).wait_send()

        @pl.when(goes_up(d))
        def _():
            for h in range(2):
                up_own(d, h, c).wait_send()
            for m in range(2):

                @pl.when(m < k)
                def _():
                    up_fwd(d, m).wait_send()

        for m in range(3):

            @pl.when(jnp.logical_and(m < k, jnp.logical_or(below_top, d >= NB)))
            def _():
                down(d, m).wait_send()

        return carry

    lax.fori_loop(0, ND, drain, 0)
    sib_w().wait_send()
    sib_dm().wait_send()

    @pl.when(top)
    def _():
        for h in range(2):
            top_w(h, c).wait_send()
            for d in range(NB):
                hand(d, h, c).wait_send()

    @pl.when(k == 2)
    def _():
        for cc in range(2):
            top_dm(cc, c).wait_send()

    def drain_peer(o, carry):
        p = around(o)
        turn(p, q).wait_send()
        tell(p, q).wait_send()
        ag(p, q).wait_send()
        return carry

    lax.fori_loop(1, nq, drain_peer, 0)
    swap().wait_send()
    for e in range(2):
        store(e).wait()


def copies(g_ref, w_ref, o_ref, n_ref, g_out, w_out, o_out, n_out, G, W, O, N, read, write):
    rows = G.shape[0] // 4
    pairs = [(g_ref.at[pl.ds(e * rows, rows)], G.at[pl.ds(e * rows, rows)], g_out.at[pl.ds(e * rows, rows)]) for e in range(4)]
    rows_w = W.shape[0] // 2
    pairs += [(w_ref.at[pl.ds(e * rows_w, rows_w)], W.at[pl.ds(e * rows_w, rows_w)], w_out.at[pl.ds(e * rows_w, rows_w)]) for e in range(2)]
    pairs += [(o_ref, O, o_out), (n_ref, N, n_out)]
    reads = [pltpu.make_async_copy(a, b, read.at[i]) for i, (a, b, _) in enumerate(pairs)]
    writes = [pltpu.make_async_copy(b, c, write.at[i]) for i, (_, b, c) in enumerate(pairs)]
    for move in reads:
        move.start()
    for i in range(len(pairs)):
        reads[i].wait()
        writes[i].start()
    for move in writes:
        move.wait()


def hand_over(*arrays):
    any_space = pl.BlockSpec(memory_space=pl.ANY)
    return pl.pallas_call(
        copies,
        out_shape=tuple(jax.ShapeDtypeStruct(a.shape, a.dtype) for a in arrays),
        in_specs=[any_space] * len(arrays),
        out_specs=(any_space,) * len(arrays),
        scratch_shapes=[pltpu.VMEM(a.shape, a.dtype) for a in arrays] + [pltpu.SemaphoreType.DMA((8,))] * 2,
        name="hand_over",
        compiler_params=pltpu.CompilerParams(vmem_limit_bytes=56 << 20),
    )(*arrays)


def shards(outputs, cotangents, gain, w_in, w_out):
    D = outputs.shape[2]
    nq = lax.axis_size("dp") // 2
    DC = D // ND
    CW = D // nq
    dma = pltpu.SemaphoreType.DMA
    any_space = pl.BlockSpec(memory_space=pl.ANY)
    vmem = pl.BlockSpec(memory_space=pltpu.VMEM)
    scratch = [
        pltpu.VMEM((128, D), BF16),
        pltpu.VMEM((128, D), BF16),
        pltpu.VMEM((128, D), BF16),
        pltpu.VMEM((128, D), F32),
        pltpu.VMEM((ND, 8, 64, DC), BF16),
        pltpu.VMEM((ND, 8, 64, DC), BF16),
        pltpu.VMEM((NB, 8, 64, DC), BF16),
        pltpu.VMEM((ND, 8, 64, DC), BF16),
        pltpu.VMEM((ND, 6, 64, DC), BF16),
        pltpu.VMEM((ND, 64, DC), BF16),
        pltpu.VMEM((2, 256, DC), F32),
        pltpu.VMEM((2, 256, 256), BF16),
        pltpu.VMEM((2, 256, 256), BF16),
        pltpu.VMEM((2, 256, 256), F32),
        pltpu.VMEM((2, 256, 256), F32),
        pltpu.VMEM((32, 128), F32),
        pltpu.VMEM((128, 1), F32),
        pltpu.VMEM((128, 1), F32),
        pltpu.VMEM((128, 128), BF16),
        pltpu.VMEM((2, 64, 128), BF16),
        pltpu.VMEM((2, 64, 128), BF16),
        pltpu.VMEM((2, 64, 128), F32),
        pltpu.VMEM((2, 64, 128), F32),
        pltpu.VMEM((2, 64, 128), F32),
        pltpu.VMEM((2, 64, 128), F32),
        pltpu.VMEM((32, 128), BF16),
        pltpu.VMEM((16, 128), F32),
        pltpu.VMEM((nq, 128, CW), BF16),
        pltpu.VMEM((48, 128), BF16),
        pltpu.VMEM((nq, 48, 128), BF16),
        pltpu.VMEM((48, CW), BF16),
        pltpu.VMEM((48, CW), BF16),
        pltpu.VMEM((nq, 32, CW), BF16),
        dma, dma((2,)), dma((ND,)), dma((ND,)),
        dma((ND,)), dma((ND,)), dma((ND,)), dma((ND,)),
        dma((ND, 2)), dma((ND, 2)), dma((ND, 2)), dma((ND, 2)),
        dma((ND, 3)), dma((ND, 3)), dma((NB, 2)), dma((NB, 2)),
        dma((ND,)), dma((ND,)), dma, dma, dma((2,)), dma((2,)),
        dma, dma, dma((2,)), dma((2,)),
        dma((nq,)), dma((nq,)), dma((nq,)), dma((nq,)),
        dma, dma, dma((nq,)), dma((nq,)),
    ]
    grad, gwin, gwout, ggain = pl.pallas_call(
        functools.partial(kernel, nq),
        out_shape=(
            jax.ShapeDtypeStruct((128, D), BF16),
            jax.ShapeDtypeStruct((32, D), F32),
            jax.ShapeDtypeStruct((32, 32), F32),
            jax.ShapeDtypeStruct((1, D), F32),
        ),
        in_specs=[any_space, any_space, vmem, vmem, vmem],
        out_specs=(any_space, vmem, vmem, vmem),
        scratch_shapes=scratch,
        name="dense_back",
        compiler_params=pltpu.CompilerParams(
            collective_id=0, has_side_effects=True, vmem_limit_bytes=56 << 20
        ),
    )(outputs[0], cotangents[0], gain, w_in[0].T, w_out[0])
    grad, gwin, gwout, ggain = hand_over(grad, gwin, gwout, ggain)
    return grad[None], gwin.T[None], gwout[None], ggain


def solution(mesh):
    placed = (
        P("section", "dp", None),
        P("section", None, "dp", None),
        P("section", None),
        P("section", None, None),
        P("section", None, None),
    )
    return jax.shard_map(
        shards,
        mesh=mesh,
        in_specs=placed,
        out_specs=(
            P("section", "dp", None),
            P("section", None, None),
            P("section", None, None),
            P("section", None),
        ),
        check_vma=False,
    )
```

```python
import functools

import jax
import jax.numpy as jnp
from jax import lax
from jax.experimental import pallas as pl
from jax.experimental.pallas import tpu as pltpu
from jax.sharding import PartitionSpec as P

ND = 8
NB = 1
PF = 3
PF_TOP = 6
MESH = pl.DeviceIdType.MESH
F32 = jnp.float32
BF16 = jnp.bfloat16
C0 = 0.7978845608028654
C1 = 0.044715


def gelu(v):
    return 0.5 * v * (1.0 + jnp.tanh(C0 * (v + C1 * v * v * v)))


def gelu_slope(v):
    t = jnp.tanh(C0 * (v + C1 * v * v * v))
    return 0.5 * (1.0 + t) + 0.5 * v * (1.0 - t * t) * (C0 * (1.0 + 3.0 * C1 * v * v))


def nt(a, b):
    return lax.dot_general(a, b, (((1,), (1,)), ((), ())), preferred_element_type=F32)


def tn(a, b):
    return lax.dot_general(a, b, (((0,), (0,)), ((), ())), preferred_element_type=F32)


def iota(shape, dim):
    return lax.broadcasted_iota(jnp.int32, shape, dim)


def kernel(
    nq, x_ref, cot_ref, gain_ref, win_ref, wout_ref,
    out_ref, gwin_ref, gwout_ref, ggain_ref,
    X, HN, OUT, GG, G, C, CB, PB, R, SR, PS, A, A3, ACC, ACC3,
    PRE, RI, MS, WF, WS, W3, DMT, DM, DMB, D3X, DP, WO,
    HT, MSG, MR, ZS, ZR, AG,
    x_sem, out_sem, lg_sem, lc_sem, sg_s, sg_r, sc_s, sc_r, up_s, up_r, fw_s, fw_r,
    dn_s, dn_r, cb_s, cb_r, ss_s, ss_r, w_s, w_r, w3_s, w3_r, dm_s, dm_r, d3_s, d3_r,
    ht_s, ht_r, ms_s, ms_r, z_s, z_r, ag_s, ag_r,
):
    D = x_ref.shape[1]
    DC = D // ND
    CW = D // nq
    s = lax.axis_index("section")
    dp = lax.axis_index("dp")
    k = s // 2
    c = s % 2
    q = dp // 2
    zh = dp % 2
    sib = s + 1 - 2 * c
    top = k == 3
    below_top = k < 3

    def half(h):
        return pl.ds(pl.multiple_of(h * 64, 64), 64)

    def cols(d):
        return pl.ds(pl.multiple_of(d * DC, 128), DC)

    def wide(p):
        return pl.ds(pl.multiple_of(p * CW, 128), CW)

    def send(src, dst, ss, rs, to):
        return pltpu.make_async_remote_copy(
            src_ref=src, dst_ref=dst, send_sem=ss, recv_sem=rs, device_id=to, device_id_type=MESH
        )

    def sec(n):
        return {"section": n}

    def load_x():
        return pltpu.make_async_copy(x_ref, X, x_sem)

    def load_g(d):
        return pltpu.make_async_copy(x_ref.at[half(c), cols(d)], G.at[d, s], lg_sem.at[d])

    def load_c(d):
        return pltpu.make_async_copy(
            cot_ref.at[:, half(c), cols(d)], C.at[d, pl.ds(4 * c, 4)], lc_sem.at[d]
        )

    def sib_g(d):
        return send(x_ref.at[half(1 - c), cols(d)], G.at[d, s], sg_s.at[d], sg_r.at[d], sec(sib))

    def sib_c(d):
        return send(
            cot_ref.at[:, half(1 - c), cols(d)], C.at[d, pl.ds(4 * c, 4)], sc_s.at[d], sc_r.at[d], sec(sib)
        )

    def up_own(d, h, source):
        to = jnp.minimum(2 * k + 2 + h, 7)
        return send(x_ref.at[half(h), cols(d)], G.at[d, s], up_s.at[d, h], up_r.at[d, source], sec(to))

    def up_fwd(d, m):
        pair = pl.ds(2 * m, 2)
        return send(
            G.at[d, pair], G.at[d, pair], fw_s.at[d, m], fw_r.at[d, m], sec(jnp.minimum(s + 2, 7))
        )

    def down(d, m):
        pair = pl.ds(2 * m, 2)
        return send(
            PB.at[d, pair], R.at[d, pair], dn_s.at[d, m], dn_r.at[d, m], sec(jnp.maximum(s - 2, 0))
        )

    def hand(d, h, source):
        return send(
            cot_ref.at[:, half(h), cols(d)], CB.at[d, pl.ds(4 * c, 4)], cb_s.at[d, h], cb_r.at[d, source],
            sec(4 + h),
        )

    def sib_s(d):
        return send(PB.at[d, sib], SR.at[d], ss_s.at[d], ss_r.at[d], sec(sib))

    def sib_w():
        return send(WF.at[half(1 - c)], WS.at[c], w_s, w_r, sec(sib))

    def top_w(h, source):
        return send(WF.at[half(h)], W3.at[c], w3_s.at[h], w3_r.at[source], sec(4 + h))

    def sib_dm():
        return send(DMT.at[1 - c], DM.at[c], dm_s, dm_r, sec(sib))

    def top_dm(cc, source):
        return send(D3X.at[cc], DMB.at[c], d3_s.at[cc], d3_r.at[source], sec(6 + cc))

    def peer(p):
        return {"dp": 2 * p + zh}

    def turn(p, source):
        return send(HN.at[:, wide(p)], HT.at[q], ht_s.at[p], ht_r.at[source], peer(p))

    def tell(p, source):
        return send(MSG, MR.at[q], ms_s.at[p], ms_r.at[source], peer(p))

    def swap():
        return send(ZS, ZR, z_s, z_r, {"dp": dp + 1 - 2 * zh})

    def ag(p, source):
        return send(AG.at[q], AG.at[q], ag_s.at[p], ag_r.at[source], peer(p))

    def around(o):
        return lax.rem(q + o, nq)

    load_x().start()

    def first_loads(d, carry):
        load_c(d).start()
        load_g(d).start()
        return carry

    lax.fori_loop(0, PF, first_loads, 0)

    barrier = pltpu.get_barrier_semaphore()

    def greet(to):
        pl.semaphore_signal(barrier, inc=1, device_id=to, device_id_type=MESH)

    greet(sec(sib))
    for h in range(2):

        @pl.when(below_top)
        def _():
            greet(sec(jnp.minimum(2 * k + 2 + h, 7)))

        @pl.when(k > 0)
        def _():
            greet(sec(jnp.maximum(2 * k - 2 + h, 0)))

    def greet_peer(o, carry):
        greet(peer(around(o)))
        return carry

    lax.fori_loop(1, nq, greet_peer, 0)
    greet({"dp": dp + 1 - 2 * zh})
    sides = jnp.where(below_top, 2, 0) + jnp.where(k > 0, 2, 0)
    pl.semaphore_wait(barrier, nq + 1 + sides)

    def goes_up(d):
        return jnp.logical_and(below_top, jnp.logical_or(k < 2, d >= NB))

    def start_up(d):
        @pl.when(goes_up(d))
        def _():
            for h in range(2):
                up_own(d, h, c).start()

    @pl.when(top)
    def _():
        for d in range(NB):
            for h in range(2):
                hand(d, h, c).start()

    def first_sends(d, carry):
        start_up(d)
        sib_c(d).start()
        sib_g(d).start()
        return carry

    lax.fori_loop(0, PF, first_sends, 0)
    ahead = jnp.where(k == 2, PF_TOP, PF)

    def more_up(d, carry):
        start_up(d)
        return carry

    lax.fori_loop(PF, ahead, more_up, 0)

    speed = jnp.where(k < 2, 4, 3)

    def used(i):
        return jnp.minimum(ND, jnp.where(top, i + 1, ((i + 1) * speed) // 2))

    @pl.when(top)
    def _():
        for d in range(NB):
            for j in range(6):
                G[d, j] = jnp.zeros((64, DC), BF16)

    load_x().wait()
    step = D // 6

    def norm_rows(r, carry):
        rows = pl.ds(pl.multiple_of(r * 16, 16), 16)
        total = jnp.zeros((16, 1), F32)
        for p in range(6):
            v = X[rows, p * step : (p + 1) * step].astype(F32)
            total = total + jnp.sum(v * v, axis=1, keepdims=True)
        rinv = lax.rsqrt(total * (1.0 / D) + 1e-06)
        RI[rows, :] = rinv
        for p in range(6):
            at = slice(p * step, (p + 1) * step)
            HN[rows, at] = (X[rows, at].astype(F32) * rinv * gain_ref[:, at]).astype(BF16)
        return carry

    lax.fori_loop(0, 8, norm_rows, 0)
    pre = nt(win_ref[...], HN[...])
    PRE[...] = pre
    mixw = tn(gelu(pre).astype(BF16), wout_ref[...])
    mixw = jnp.where((iota((128, 32), 1) & 7) <= s, mixw, 0.0)
    WF[...] = jnp.zeros((128, 128), BF16)
    WF[:, 0:32] = mixw.astype(BF16)
    sib_w().start()

    @pl.when(top)
    def _():
        for h in range(2):
            top_w(h, c).start()

    WS[c] = WF[half(c), :]
    for g in range(2):
        ACC[g] = jnp.zeros((256, 256), F32)
    sib_w().wait_recv()

    def spread(W, A):
        row = iota((256, 128), 0)
        lane = iota((256, 128), 1)
        pick = jnp.logical_and(lane < 32, (lane & 7) == (row >> 5))
        srow = iota((128, 256), 0)
        scol = iota((128, 256), 1)
        same = (iota((256, 256), 0) & 31) == (iota((256, 256), 1) & 31)
        for g in range(2):
            total = jnp.zeros((256, 256), F32)
            for cc in range(2):
                w = W[cc, 32 * g : 32 * g + 32, :].astype(F32)
                w = jnp.where(pick, jnp.concatenate([w] * 8, axis=0), 0.0).astype(BF16)
                place = jnp.logical_and(srow < 32, (scol >> 5) == 4 * cc + (srow >> 3))
                total = total + jnp.dot(w, jnp.where(place, 1.0, 0.0).astype(BF16), preferred_element_type=F32)
            A[g] = jnp.where(same, total, 0.0).astype(BF16)

    spread(WS, A)
    HT[q] = HN[:, wide(q)]

    def start_turn(o, carry):
        turn(around(o), q).start()
        return carry

    lax.fori_loop(1, nq, start_turn, 0)

    def group(ref, d, g):
        return ref[d, :, 32 * g : 32 * g + 32, :].reshape(256, DC)

    def stage_part(d):
        handed = d < NB

        @pl.when(top)
        def _():
            load_c(d).wait()
            sib_c(d).wait_recv()

        for g in range(2):
            PS[g] = jnp.dot(A[g], group(C, d, g), preferred_element_type=F32)

        @pl.when(jnp.logical_and(k == 2, handed))
        def _():
            @pl.when(d == 0)
            def _():
                for a in range(2):
                    top_w(0, a).wait_recv()
                spread(W3, A3)
                for g in range(2):
                    ACC3[g] = jnp.zeros((256, 256), F32)

            for a in range(2):
                hand(d, 0, a).wait_recv()
            for g in range(2):
                PS[g] = PS[g] + jnp.dot(A3[g], group(CB, d, g), preferred_element_type=F32)
                ACC3[g] = ACC3[g] + nt(group(CB, d, g), group(G, d, g))

        takes = jnp.logical_and(below_top, jnp.logical_or(k < 2, d >= NB))
        for m in range(4):

            def keep(with_r):
                for g in range(2):
                    rows = slice(32 * g, 32 * g + 32)
                    own = PS[g, 64 * m : 64 * m + 64, :].reshape(2, 32, DC)
                    if with_r:
                        own = own + R[d, 2 * m : 2 * m + 2, rows, :].astype(F32)
                    PB[d, 2 * m : 2 * m + 2, rows, :] = own.astype(BF16)

            if m < 3:

                @pl.when(jnp.logical_and(m <= k, takes))
                def _():
                    down(d, m).wait_recv()
                    keep(True)

            @pl.when(jnp.logical_and(m <= k, jnp.logical_not(takes)))
            def _():
                keep(False)

            if m < 3:

                @pl.when(jnp.logical_and(m < k, jnp.logical_or(below_top, d >= NB)))
                def _():
                    down(d, m).start()

            @pl.when(m == k)
            def _():
                sib_s(d).start()

    def stage_gather(d):
        for m in (2, 1, 0):

            @pl.when(jnp.logical_and(m < k, jnp.logical_or(below_top, d >= NB)))
            def _():
                @pl.when(m == k - 1)
                def _():
                    for a in range(2):
                        up_own(d, 0, a).wait_recv()

                if m < 2:

                    @pl.when(m < k - 1)
                    def _():
                        up_fwd(d, m).wait_recv()

                    @pl.when(goes_up(d))
                    def _():
                        up_fwd(d, m).start()

    def stage_dmix(d):
        @pl.when(below_top)
        def _():
            load_c(d).wait()
            sib_c(d).wait_recv()

        load_g(d).wait()
        sib_g(d).wait_recv()
        for g in range(2):
            ACC[g] = ACC[g] + nt(group(C, d, g), group(G, d, g))

    def extract(acc, low, rise, into):
        row = iota((256, 256), 0)
        col = iota((256, 256), 1)
        ok = jnp.logical_and((row & 31) == (col & 31), (col >> 5) <= low + rise * (row >> 7))
        srow = iota((256, 128), 0)
        lane = iota((256, 128), 1)
        place = jnp.where(jnp.logical_and(lane < 32, (lane & 7) == (srow >> 5)), 1.0, 0.0)
        mine = (lane >> 3) == ((srow >> 5) & 3)
        for g in range(2):
            v = jnp.where(ok, acc[g], 0.0)
            v = jnp.dot(v, place, precision=lax.Precision.HIGHEST, preferred_element_type=F32)
            v = jnp.where(mine, v, 0.0)
            for cc in range(2):
                into[cc, 32 * g : 32 * g + 32, :] = sum(
                    v[128 * cc + 32 * st : 128 * cc + 32 * st + 32] for st in range(4)
                )

    def stage_grads():
        extract(ACC, 2 * k, 1, DMT)
        sib_dm().start()
        DM[c] = DMT[c]
        sib_dm().wait_recv()

        @pl.when(top)
        def _():
            for a in range(2):
                top_dm(0, a).wait_recv()
            DM[...] = DM[...] + DMB[...]

        dflat = DM[...].reshape(128, 128)[:, 0:32].astype(BF16)
        pre = PRE[...]
        dpre = (gelu_slope(pre) * nt(wout_ref[...], dflat)).astype(BF16)
        DP[...] = dpre
        wgrad = jnp.dot(gelu(pre).astype(BF16), dflat, preferred_element_type=F32)
        MSG[0:32, :] = dpre
        MSG[32:48, :] = jnp.zeros((16, 128), BF16)
        MSG[32:48, 0:32] = wgrad[0:16].astype(BF16)
        MSG[32:48, 32:64] = wgrad[16:32].astype(BF16)
        MR[q] = MSG[...]

        def give(o, carry):
            tell(around(o), q).start()
            return carry

        lax.fori_loop(1, nq, give, 0)
        along = lax.dot_general(
            pre * dpre.astype(F32), jnp.ones((32, 128), F32), (((0,), (0,)), ((), ())),
            precision=lax.Precision.HIGHEST, preferred_element_type=F32,
        )
        MS[...] = along[:, 0:1] * (1.0 / D)
        gates(0, part)

    part = nq // 3

    def gates(lo, hi):
        def gate(p, carry):
            at = wide(p)
            dn = tn(DP[...], win_ref[:, at]) * gain_ref[:, at]
            normed = X[:, at].astype(F32) * RI[...]
            GG[:, at] = RI[...] * (dn - normed * MS[...])
            return carry

        lax.fori_loop(lo, hi, gate, 0)

    def stage_sum():
        def hear(o, carry):
            p = around(o)
            turn(0, p).wait_recv()
            tell(0, p).wait_recv()
            return carry

        lax.fori_loop(1, nq, hear, 0)
        told = jnp.concatenate([MR[p, 0:32, :] for p in range(nq)], axis=1)
        ZS[0:32, :] = jnp.dot(told, HT[...].reshape(nq * 128, CW), preferred_element_type=F32).astype(BF16)
        wgrad = sum(MR[p, 32:48, :].astype(F32) for p in range(nq))
        ZS[32:48, :] = jnp.zeros((16, CW), BF16)
        ZS[32:48, 0:128] = wgrad.astype(BF16)
        swap().start()
        gates(part, 2 * part)

    def stage_share():
        swap().wait_recv()
        both = ZS[...].astype(F32) + ZR[...].astype(F32)
        AG[q] = both[0:32].astype(BF16)

        def give(o, carry):
            ag(around(o), q).start()
            return carry

        lax.fori_loop(1, nq, give, 0)
        WO[...] = both[32:48, 0:128]
        gates(2 * part, nq)

    def finish(d, carry):
        sib_s(d).wait_recv()
        at = cols(d)
        OUT[half(c), at] = (PB[d, s].astype(F32) + GG[half(c), at]).astype(BF16)
        OUT[half(1 - c), at] = (SR[d].astype(F32) + GG[half(1 - c), at]).astype(BF16)
        return carry

    early = 3 * ND // 4

    def store(e):
        at = slice(0, early * DC) if e == 0 else slice(early * DC, D)
        return pltpu.make_async_copy(OUT.at[:, at], out_ref.at[:, at], out_sem.at[e])

    def stage_finish():
        lax.fori_loop(0, early, finish, 0)
        store(0).start()

    lead_part = jnp.where(top, 0, 1)
    tail = jnp.where(top, 2 * ND, (2 * ND + 2) // 3)

    def body(i, carry):
        def loads(d, carry):
            load_c(d).start()
            load_g(d).start()
            sib_c(d).start()
            sib_g(d).start()
            return carry

        lax.fori_loop(jnp.minimum(ND, used(i - 1) + PF), jnp.minimum(ND, used(i) + PF), loads, 0)
        lax.fori_loop(jnp.minimum(ND, used(i - 1) + ahead), jnp.minimum(ND, used(i) + ahead), more_up, 0)

        @pl.when(jnp.logical_and(k == 2, i == NB + 1))
        def _():
            extract(ACC3, 5, 0, D3X)
            for cc in range(2):
                top_dm(cc, c).start()

        pl.when(i == tail)(stage_grads)
        pl.when(i == tail + 1)(stage_sum)
        pl.when(i == tail + 2)(stage_share)
        pl.when(i == tail + 2)(stage_finish)
        d = i - lead_part

        @pl.when(jnp.logical_and(d >= 0, d < ND))
        def _():
            stage_part(d)

        def dots(d, carry):
            stage_gather(d)
            stage_dmix(d)
            return carry

        lo = jnp.where(top, jnp.clip(i - ND, 0, ND), used(i - 1))
        hi = jnp.where(top, jnp.clip(i - ND + 1, 0, ND), used(i))
        lax.fori_loop(lo, hi, dots, 0)
        return carry

    lax.fori_loop(0, 2 * ND + 3, body, 0)

    lax.fori_loop(early, ND, finish, 0)
    store(1).start()

    def unpack(o, carry):
        p = around(o)

        @pl.when(o < nq)
        def _():
            ag(0, p).wait_recv()

        at = wide(p)
        m = AG[p].astype(F32)
        gwin_ref[:, at] = m
        ggain_ref[:, at] = jnp.sum(m * win_ref[:, at].astype(F32), axis=0, keepdims=True) / gain_ref[:, at]
        return carry

    lax.fori_loop(1, nq + 1, unpack, 0)
    gwout_ref[0:16, :] = WO[:, 0:32]
    gwout_ref[16:32, :] = WO[:, 32:64]

    def drain(d, carry):
        sib_c(d).wait_send()
        sib_g(d).wait_send()
        sib_s(d).wait_send()

        @pl.when(goes_up(d))
        def _():
            for h in range(2):
                up_own(d, h, c).wait_send()
            for m in range(2):

                @pl.when(m < k)
                def _():
                    up_fwd(d, m).wait_send()

        for m in range(3):

            @pl.when(jnp.logical_and(m < k, jnp.logical_or(below_top, d >= NB)))
            def _():
                down(d, m).wait_send()

        return carry

    lax.fori_loop(0, ND, drain, 0)
    sib_w().wait_send()
    sib_dm().wait_send()

    @pl.when(top)
    def _():
        for h in range(2):
            top_w(h, c).wait_send()
            for d in range(NB):
                hand(d, h, c).wait_send()

    @pl.when(k == 2)
    def _():
        for cc in range(2):
            top_dm(cc, c).wait_send()

    def drain_peer(o, carry):
        p = around(o)
        turn(p, q).wait_send()
        tell(p, q).wait_send()
        ag(p, q).wait_send()
        return carry

    lax.fori_loop(1, nq, drain_peer, 0)
    swap().wait_send()
    for e in range(2):
        store(e).wait()


def copies(g_ref, w_ref, o_ref, n_ref, g_out, w_out, o_out, n_out, G, W, O, N, read, write):
    rows = G.shape[0] // 8
    pairs = [(g_ref.at[pl.ds(e * rows, rows)], G.at[pl.ds(e * rows, rows)], g_out.at[pl.ds(e * rows, rows)]) for e in range(8)]
    rows_w = W.shape[0] // 4
    pairs += [(w_ref.at[pl.ds(e * rows_w, rows_w)], W.at[pl.ds(e * rows_w, rows_w)], w_out.at[pl.ds(e * rows_w, rows_w)]) for e in range(4)]
    pairs += [(o_ref, O, o_out), (n_ref, N, n_out)]
    reads = [pltpu.make_async_copy(a, b, read.at[i]) for i, (a, b, _) in enumerate(pairs)]
    writes = [pltpu.make_async_copy(b, c, write.at[i]) for i, (_, b, c) in enumerate(pairs)]
    for move in reads:
        move.start()
    for i in range(len(pairs)):
        reads[i].wait()
        writes[i].start()
    for move in writes:
        move.wait()


def hand_over(*arrays):
    any_space = pl.BlockSpec(memory_space=pl.ANY)
    return pl.pallas_call(
        copies,
        out_shape=tuple(jax.ShapeDtypeStruct(a.shape, a.dtype) for a in arrays),
        in_specs=[any_space] * len(arrays),
        out_specs=(any_space,) * len(arrays),
        scratch_shapes=[pltpu.VMEM(a.shape, a.dtype) for a in arrays] + [pltpu.SemaphoreType.DMA((14,))] * 2,
        name="hand_over",
        compiler_params=pltpu.CompilerParams(vmem_limit_bytes=56 << 20),
    )(*arrays)


def shards(outputs, cotangents, gain, w_in, w_out):
    D = outputs.shape[2]
    nq = lax.axis_size("dp") // 2
    DC = D // ND
    CW = D // nq
    dma = pltpu.SemaphoreType.DMA
    any_space = pl.BlockSpec(memory_space=pl.ANY)
    vmem = pl.BlockSpec(memory_space=pltpu.VMEM)
    scratch = [
        pltpu.VMEM((128, D), BF16),
        pltpu.VMEM((128, D), BF16),
        pltpu.VMEM((128, D), BF16),
        pltpu.VMEM((128, D), F32),
        pltpu.VMEM((ND, 8, 64, DC), BF16),
        pltpu.VMEM((ND, 8, 64, DC), BF16),
        pltpu.VMEM((NB, 8, 64, DC), BF16),
        pltpu.VMEM((ND, 8, 64, DC), BF16),
        pltpu.VMEM((ND, 6, 64, DC), BF16),
        pltpu.VMEM((ND, 64, DC), BF16),
        pltpu.VMEM((2, 256, DC), F32),
        pltpu.VMEM((2, 256, 256), BF16),
        pltpu.VMEM((2, 256, 256), BF16),
        pltpu.VMEM((2, 256, 256), F32),
        pltpu.VMEM((2, 256, 256), F32),
        pltpu.VMEM((32, 128), F32),
        pltpu.VMEM((128, 1), F32),
        pltpu.VMEM((128, 1), F32),
        pltpu.VMEM((128, 128), BF16),
        pltpu.VMEM((2, 64, 128), BF16),
        pltpu.VMEM((2, 64, 128), BF16),
        pltpu.VMEM((2, 64, 128), F32),
        pltpu.VMEM((2, 64, 128), F32),
        pltpu.VMEM((2, 64, 128), F32),
        pltpu.VMEM((2, 64, 128), F32),
        pltpu.VMEM((32, 128), BF16),
        pltpu.VMEM((16, 128), F32),
        pltpu.VMEM((nq, 128, CW), BF16),
        pltpu.VMEM((48, 128), BF16),
        pltpu.VMEM((nq, 48, 128), BF16),
        pltpu.VMEM((48, CW), BF16),
        pltpu.VMEM((48, CW), BF16),
        pltpu.VMEM((nq, 32, CW), BF16),
        dma, dma((2,)), dma((ND,)), dma((ND,)),
        dma((ND,)), dma((ND,)), dma((ND,)), dma((ND,)),
        dma((ND, 2)), dma((ND, 2)), dma((ND, 2)), dma((ND, 2)),
        dma((ND, 3)), dma((ND, 3)), dma((NB, 2)), dma((NB, 2)),
        dma((ND,)), dma((ND,)), dma, dma, dma((2,)), dma((2,)),
        dma, dma, dma((2,)), dma((2,)),
        dma((nq,)), dma((nq,)), dma((nq,)), dma((nq,)),
        dma, dma, dma((nq,)), dma((nq,)),
    ]
    grad, gwin, gwout, ggain = pl.pallas_call(
        functools.partial(kernel, nq),
        out_shape=(
            jax.ShapeDtypeStruct((128, D), BF16),
            jax.ShapeDtypeStruct((32, D), F32),
            jax.ShapeDtypeStruct((32, 32), F32),
            jax.ShapeDtypeStruct((1, D), F32),
        ),
        in_specs=[any_space, any_space, vmem, vmem, vmem],
        out_specs=(any_space, vmem, vmem, vmem),
        scratch_shapes=scratch,
        name="dense_back",
        compiler_params=pltpu.CompilerParams(
            collective_id=0, has_side_effects=True, vmem_limit_bytes=56 << 20
        ),
    )(outputs[0], cotangents[0], gain, w_in[0].T, w_out[0])
    grad, gwin, gwout, ggain = hand_over(grad, gwin, gwout, ggain)
    return grad[None], gwin.T[None], gwout[None], ggain


def solution(mesh):
    placed = (
        P("section", "dp", None),
        P("section", None, "dp", None),
        P("section", None),
        P("section", None, None),
        P("section", None, None),
    )
    return jax.shard_map(
        shards,
        mesh=mesh,
        in_specs=placed,
        out_specs=(
            P("section", "dp", None),
            P("section", None, None),
            P("section", None, None),
            P("section", None),
        ),
        check_vma=False,
    )
```
